512 devices in a mesh: seq: 16 (over y, x), mp: 32 (over z, core).
Axes of the slice: x: 4, y: 4, z: 16, core: 2. Of those that a mesh axis runs over, the one named last changes fastest.
Arguments:
- queries: bfloat16 [2048, 8192], P('seq', 'mp'), may hold values from -3 to 3
- key_rows: bfloat16 [2048, 8192], P('seq', 'mp'), may hold values from -1.25 to 1.25
- value_rows: bfloat16 [2048, 8192], P('seq', 'mp'), may hold values from -4 to 4
- decay_rates: float32 [64], P('mp'), may hold values from 5e-05 to 0.001
- w_out: bfloat16 [8192, 3072], P('mp'), may hold values from -0.125 to 0.125
- inputs: bfloat16 [2048, 3072], P(('seq', 'mp')), may hold values from -4 to 4
- cotangent: bfloat16 [2048, 3072], P(('seq', 'mp')), may hold values from -6 to 6
- norm_gain: float32 [3072], replicated, may hold values from 0.5 to 1.5
- expert_ids: int32 [2048, 2], P('seq'), may hold values from 0 to 15, all different within a row; in each aligned block of 128 rows (0 to 127, 128 to 255, ...) at most 32 rows name the same one
- gate_weights: float32 [2048, 2], P('seq'), may hold values from 0.1 to 0.9
- w_gate: bfloat16 [16, 3072, 4608], P('seq', None, 'mp'), may hold values from -0.109375 to 0.109375
- w_up: bfloat16 [16, 3072, 4608], P('seq', None, 'mp'), may hold values from -0.109375 to 0.109375
- w_down: bfloat16 [16, 4608, 3072], P('seq', 'mp'), may hold values from -0.09375 to 0.09375
Outputs:
- query_grad: bfloat16 [2048, 8192], P('seq', 'mp')
- key_grad: bfloat16 [2048, 8192], P('seq', 'mp')
- value_grad: bfloat16 [2048, 8192], P('seq', 'mp')
- input_grad: bfloat16 [2048, 3072], P(('seq', 'mp'))
The draws below stay inside these ranges and needn't reach their ends.
Inputs may be any that keep to these rules, and one draw needn't show every extreme that they name: `expert_ids`: A token's two experts differ. Among the 128 tokens of one index of seq no expert is named by more than 32 tokens, a bound that some block reaches.
All inputs are finite; a program needn't handle non-finite values.
Results may differ from the reference program's by a relative error of at most 0.025.
Values may be sent and summed in bfloat16 or wider, within the bound.
No kernel may reach another device: no remote copies, remote signals or barrier semaphores. Data moves between devices by JAX's collectives and lax.ppermute only.
A program may use at most 64 MiB of HBM per device.

```python
import math
import jax
import jax.numpy as jnp
import numpy as np
from jax import lax

D = 3072
HD = 128
HEADS_DEV = 2
HEADS = 64
EXP_FF = 4608
TOK_DEV = 128
TOKENS = 2048
EXPERTS = 16
CAPG = 32
N_SEQ = 16
N_MP = 32


def strengthened(result, stream_key, source, target, blocks, factor):
    def block_of(axis_at):
        return (jnp.arange(result.shape[axis_at]) // (result.shape[axis_at] // blocks)).reshape((-1,) + (1,) * (result.ndim - 1 - axis_at))

    near = jax.random.permutation(stream_key, blocks)[block_of(target)]
    other_side = (block_of(target) + blocks // 2) % blocks
    return jnp.where((block_of(source) == near) | (block_of(source) == other_side), factor * result, result)


def levels(stream_key, extent, cuts, least, largest):
    def one(dim, blocks):
        steps = jax.random.uniform(jax.random.fold_in(jax.random.fold_in(stream_key, 6), dim), (blocks,), jnp.float32, least / len(cuts), largest / len(cuts))
        return jnp.repeat(jnp.exp(steps), extent[dim] // blocks).reshape((-1,) + (1,) * (len(extent) - dim - 1))

    loudness = one(*cuts[0])
    for cut in cuts[1:]:
        loudness = loudness * one(*cut)
    return loudness


def deal_out(key, own, number, rows, count, top, limit, slope):
    order = jax.random.permutation(key, count)
    heavy_load, common = portions_of(count, rows * top, limit, slope, True), portions_of(count, rows * top, limit, slope, False)
    places = jnp.arange(count)

    def named(tallies, offset_by):
        used = int((tallies > 0).sum())
        fixed = max(1, used // 4)
        moved = fixed + (places - fixed + offset_by * (used - fixed)) % max(1, count - fixed)
        return jnp.zeros((count,), jnp.int32).at[order[jnp.where(places < fixed, places, moved)]].set(jnp.asarray(tallies, jnp.int32))

    tallies = jnp.where(number % 4 == 0, named(heavy_load, number // 4), named(common, number - number // 4 - 1))
    mixed = jax.random.permutation(jax.random.fold_in(own, 3), count)
    giver, taker = mixed[0:count // 2 * 2:2], mixed[1:count // 2 * 2:2]
    margin = jnp.minimum(tallies[giver] - 1, limit - tallies[taker]) // 2
    margin = jnp.where((giver == order[0]) | (taker == order[0]) | (tallies[taker] == 0), 0, jnp.maximum(margin, 0))
    moved = jax.random.randint(jax.random.fold_in(own, 4), (count // 2,), 0, 1 << 20) % (margin + 1)
    tallies = tallies.at[giver].add(-moved).at[taker].add(moved)
    labels = jnp.searchsorted(jnp.cumsum(tallies), jnp.arange(rows * top), side="right").astype(jnp.int32)
    listing = labels.reshape(top, rows).T
    listing = listing[jax.random.permutation(jax.random.fold_in(own, 1), rows)]
    offset_by = jax.random.randint(jax.random.fold_in(own, 2), (rows, 1), 0, top)
    return jnp.take_along_axis(listing, (jnp.arange(top)[None, :] + offset_by) % top, axis=1)


def portions_of(amount, total, bound, lean, full):
    loads = [(1 << 20) // math.isqrt(grade ** lean) + 1 for grade in range(1, amount + 1)]
    largest = bound if full else min(bound, max(-(-total // amount), total * loads[0] // sum(loads)))
    least = 1 if total - largest >= amount - 1 else 0
    given, spare = [largest] + [least] * (amount - 1), total - largest - least * (amount - 1)
    while spare > 0:
        free = [i for i in range(1, amount) if given[i] < largest] or [i for i in range(1, amount) if given[i] < bound]
        mass, budget = sum([loads[i] for i in free]), spare
        for i in free:
            more = min(bound - given[i], max(1, budget * loads[i] // mass), spare)
            given[i] = given[i] + more
            spare = spare - more
    return np.array(given)


def normal_values(key, extent, width, limit, split=(), kind=jnp.bfloat16):
    loudness = levels(key, extent, split, -0.22, 0.18) if split else 1.0
    entries = jax.random.normal(key, extent, jnp.float32) * width * loudness
    return jnp.minimum(jnp.maximum(entries, -limit), limit).astype(kind)


def bell_draw_with(key, dims, width, most, split, heavy, kind=jnp.bfloat16):
    values = width * jax.random.normal(key, dims, jnp.float32)
    if split:
        values = values * levels(key, dims, split, -0.22, 0.18)
    return jnp.clip(strengthened(values, jax.random.fold_in(key, 3), *heavy), -most, most).astype(kind)


def setup_inputs(seed: int = 0) -> dict:
    arg_keys = jax.random.split(jax.random.key(seed), 14)
    queries = normal_values(arg_keys[0], (TOKENS, HEADS * HD), 0.2, 3.0, ((0, 16), (1, 32)))
    key_rows = normal_values(arg_keys[1], (TOKENS, HEADS * HD), 0.08, 1.25, ((0, 16), (1, 32)))
    value_rows = normal_values(arg_keys[2], (TOKENS, HEADS * HD), 0.25, 4.0, ((0, 16), (1, 32)))
    decay_rates = jnp.clip(jnp.exp(math.log(0.001) - 2.9957323 * jax.random.uniform(arg_keys[3], (HEADS,), jnp.float32) ** levels(arg_keys[3], (HEADS,), ((0, 32),), -0.2, 0.2)), 4.999999873689376e-05, 0.001)
    w_out = bell_draw_with(arg_keys[4], (HEADS * HD, D), (HEADS * HD) ** -0.5, 0.125, ((0, 32),), (0, 1, 32, 2.75))
    inputs = normal_values(arg_keys[5], (TOKENS, D), 0.3, 4.0, ((0, 512),))
    cotangent = normal_values(arg_keys[6], (TOKENS, D), 1.0, 6.0, ((0, 512),))
    norm_gain = jnp.clip(1.0 + 0.1 * jax.random.normal(arg_keys[7], (D,), jnp.float32), 0.5, 1.5)
    expert_ids_keys = jax.random.split(jax.random.fold_in(arg_keys[8], 1), TOKENS // TOK_DEV)
    expert_ids_turns = jax.random.permutation(jax.random.fold_in(arg_keys[8], 3), TOKENS // TOK_DEV)
    expert_ids = jax.vmap(lambda own, number: deal_out(jax.random.fold_in(arg_keys[8], 2), own, number, TOK_DEV, EXPERTS, 2, CAPG, 2))(expert_ids_keys, expert_ids_turns).reshape((TOKENS, 2))
    gate_weights = jnp.clip(0.1 + 0.79999997 * jax.random.uniform(arg_keys[9], (TOKENS, 2), jnp.float32) ** levels(arg_keys[9], (TOKENS, 2), ((0, 16),), -0.2, 0.2), 0.1, 0.9)
    w_gate = normal_values(arg_keys[10], (EXPERTS, D, EXP_FF), D ** -0.5, 0.109375, ((0, 16), (2, 32)))
    w_up = normal_values(arg_keys[11], (EXPERTS, D, EXP_FF), D ** -0.5, 0.109375, ((0, 16), (2, 32)))
    w_down = normal_values(arg_keys[12], (EXPERTS, EXP_FF, D), EXP_FF ** -0.5, 0.09375, ((0, 16), (1, 32)))
    return dict(queries=queries, key_rows=key_rows, value_rows=value_rows, decay_rates=decay_rates, w_out=w_out, inputs=inputs, cotangent=cotangent, norm_gain=norm_gain, expert_ids=expert_ids, gate_weights=gate_weights, w_gate=w_gate, w_up=w_up, w_down=w_down)


EPSILON = 1e-06
HIGHEST_PRECISION = lax.Precision.HIGHEST

def decay_tables(decay_rates, length):
    places = jnp.arange(length).astype(jnp.float32)
    offset = places[:, None] - places[None, :]
    causal = offset >= 0
    clipped = jnp.where(causal, offset, 0.0)
    decay_band = jnp.where(causal[None], jnp.exp(-decay_rates[:, None, None] * clipped[None]), 0.0)
    head_decay = jnp.exp(-decay_rates[:, None] * places[None, :])
    tail_decay = jnp.exp(-decay_rates[:, None] * (length - 1.0 - places)[None, :])
    return (decay_band, head_decay, tail_decay)

def expert_backward(rows_in, rows_cot, gate_block, up_block, down_block):
    gate_pre = jnp.dot(rows_in, gate_block, preferred_element_type=jnp.float32)
    up_pre = jnp.dot(rows_in, up_block, preferred_element_type=jnp.float32)
    hidden_grad = lax.dot_general(rows_cot, down_block, (((1,), (1,)), ((), ())), preferred_element_type=jnp.float32)
    sigma = jax.nn.sigmoid(gate_pre)
    gate_grad = (hidden_grad * up_pre * sigma * (1.0 + gate_pre * (1.0 - sigma))).astype(jnp.bfloat16)
    up_grad = (hidden_grad * gate_pre * sigma).astype(jnp.bfloat16)
    shard_width = EXP_FF // N_MP

    def add_shard(position, running):
        first_col = (position * shard_width).astype(jnp.int32)
        gate_part = lax.dynamic_slice_in_dim(gate_grad, first_col, shard_width, 1)
        up_part = lax.dynamic_slice_in_dim(up_grad, first_col, shard_width, 1)
        gate_cols = lax.dynamic_slice_in_dim(gate_block, first_col, shard_width, 1)
        up_cols = lax.dynamic_slice_in_dim(up_block, first_col, shard_width, 1)
        partial_value = lax.dot_general(gate_part, gate_cols, (((1,), (1,)), ((), ())), preferred_element_type=jnp.float32)
        partial_value = partial_value + lax.dot_general(up_part, up_cols, (((1,), (1,)), ((), ())), preferred_element_type=jnp.float32)
        rounded = lax.optimization_barrier(partial_value.astype(jnp.bfloat16))
        return running + rounded.astype(jnp.float32)
    return lax.fori_loop(0, N_MP, add_shard, jnp.zeros((rows_in.shape[0], D), jnp.float32))

def reference(queries, key_rows, value_rows, decay_rates, w_out, inputs, cotangent, norm_gain, expert_ids, gate_weights, w_gate, w_up, w_down):
    head_count = decay_rates.shape[0]

    def to_heads(matrix):
        return matrix.astype(jnp.float32).reshape(N_SEQ, TOK_DEV, head_count, HD).transpose(0, 2, 1, 3)

    def from_heads(blocks):
        return blocks.transpose(0, 2, 1, 3).reshape(TOKENS, head_count * HD)
    query_blocks = to_heads(queries)
    key_blocks = to_heads(key_rows)
    value_blocks = to_heads(value_rows)
    decay_band, head_decay, tail_decay = decay_tables(decay_rates, TOK_DEV)
    block_decay = jnp.exp(-decay_rates * TOK_DEV)
    step_decay = jnp.exp(-decay_rates)
    zero_state = jnp.zeros((head_count, HD, HD), jnp.float32)

    def forward_turn(carried, blocks):
        query_block, key_block, value_block = blocks
        scores = jnp.einsum('htd,hsd->hts', query_block, key_block, precision=HIGHEST_PRECISION) * decay_band
        inside = jnp.einsum('hts,hse->hte', scores, value_block, precision=HIGHEST_PRECISION)
        outside = head_decay[:, :, None] * jnp.einsum('htd,hde->hte', query_block, carried, precision=HIGHEST_PRECISION)
        contribution = jnp.einsum('ht,htd,hte->hde', step_decay[:, None] * tail_decay, key_block, value_block, precision=HIGHEST_PRECISION)
        return (block_decay[:, None, None] * carried + contribution, (inside + outside, carried))
    _, (attended, entering) = lax.scan(forward_turn, zero_state, (query_blocks, key_blocks, value_blocks))
    attended_b = from_heads(attended).astype(jnp.bfloat16)
    grouped = attended_b.reshape(TOKENS, N_MP, HEADS_DEV * HD)
    out_groups = w_out.reshape(N_MP, HEADS_DEV * HD, D)

    def add_group(position, running):
        group_rows = lax.dynamic_index_in_dim(grouped, position, 1, keepdims=False)
        group_weight = lax.dynamic_index_in_dim(out_groups, position, 0, keepdims=False)
        partial_value = jnp.dot(group_rows, group_weight, preferred_element_type=jnp.float32)
        rounded = lax.optimization_barrier(partial_value.astype(jnp.bfloat16))
        return running + rounded.astype(jnp.float32)
    mixed = lax.fori_loop(0, N_MP, add_group, jnp.zeros((TOKENS, D), jnp.float32))
    stream = inputs.astype(jnp.float32) + mixed
    inverse = lax.rsqrt(lax.optimization_barrier(jnp.mean(stream * stream, axis=1, keepdims=True)) + EPSILON)
    normed = stream * inverse
    expert_in = (normed * norm_gain).astype(jnp.bfloat16)
    capacity = N_SEQ * CAPG
    token_places = jnp.arange(TOKENS, dtype=jnp.int32)
    padded_in = jnp.concatenate([expert_in, jnp.zeros((1, D), jnp.bfloat16)], axis=0)
    cot_float = cotangent.astype(jnp.float32)

    def expert_turn(running, expert):
        first_pick = expert_ids[:, 0] == expert
        second_pick = expert_ids[:, 1] == expert
        chosen = first_pick | second_pick
        weight = jnp.where(first_pick, gate_weights[:, 0], 0.0) + jnp.where(second_pick, gate_weights[:, 1], 0.0)
        ranking = jnp.cumsum(chosen.astype(jnp.int32)) - 1
        target = jnp.where(chosen, ranking, capacity).astype(jnp.int32)
        row_token = jnp.full((capacity,), TOKENS, jnp.int32).at[target].set(token_places, mode='drop')
        weighted = (weight[:, None] * cot_float).astype(jnp.bfloat16)
        padded_cot = jnp.concatenate([weighted, jnp.zeros((1, D), jnp.bfloat16)], axis=0)
        rows_in = jnp.take(padded_in, row_token, axis=0)
        rows_cot = jnp.take(padded_cot, row_token, axis=0)
        gate_block = lax.dynamic_index_in_dim(w_gate, expert, 0, keepdims=False)
        up_block = lax.dynamic_index_in_dim(w_up, expert, 0, keepdims=False)
        down_block = lax.dynamic_index_in_dim(w_down, expert, 0, keepdims=False)
        pick_sum = expert_backward(rows_in, rows_cot, gate_block, up_block, down_block)
        pick_grad = lax.optimization_barrier(pick_sum.astype(jnp.bfloat16)).astype(jnp.float32)
        return (running.at[row_token].add(pick_grad), None)
    gathered, _ = lax.scan(expert_turn, jnp.zeros((TOKENS + 1, D), jnp.float32), jnp.arange(EXPERTS, dtype=jnp.int32))
    scaled = gathered[:TOKENS] * norm_gain
    stream_grad = inverse * (scaled - normed * lax.optimization_barrier(jnp.mean(scaled * normed, axis=1, keepdims=True))) + cot_float
    input_grad = stream_grad.astype(jnp.bfloat16)
    attended_grad = lax.dot_general(input_grad, w_out, (((1,), (1,)), ((), ())), preferred_element_type=jnp.float32)
    grad_blocks = to_heads(attended_grad)

    def backward_turn(carried, blocks):
        query_block, key_block, value_block, grad_block, entering_block = blocks
        grad_scores = jnp.einsum('hte,hse->hts', grad_block, value_block, precision=HIGHEST_PRECISION) * decay_band
        scores = jnp.einsum('htd,hsd->hts', query_block, key_block, precision=HIGHEST_PRECISION) * decay_band
        query_part = jnp.einsum('hts,hsd->htd', grad_scores, key_block, precision=HIGHEST_PRECISION)
        query_part = query_part + head_decay[:, :, None] * jnp.einsum('hte,hde->htd', grad_block, entering_block, precision=HIGHEST_PRECISION)
        key_part = jnp.einsum('hts,htd->hsd', grad_scores, query_block, precision=HIGHEST_PRECISION)
        key_part = key_part + tail_decay[:, :, None] * jnp.einsum('hse,hde->hsd', value_block, carried, precision=HIGHEST_PRECISION)
        value_part = jnp.einsum('hts,hte->hse', scores, grad_block, precision=HIGHEST_PRECISION)
        value_part = value_part + tail_decay[:, :, None] * jnp.einsum('hsd,hde->hse', key_block, carried, precision=HIGHEST_PRECISION)
        contribution = jnp.einsum('ht,htd,hte->hde', step_decay[:, None] * head_decay, query_block, grad_block, precision=HIGHEST_PRECISION)
        return (block_decay[:, None, None] * carried + contribution, (query_part, key_part, value_part))
    _, (query_parts, key_parts, value_parts) = lax.scan(backward_turn, zero_state, (query_blocks, key_blocks, value_blocks, grad_blocks, entering), reverse=True)
    query_grad = from_heads(query_parts).astype(jnp.bfloat16)
    key_grad = from_heads(key_parts).astype(jnp.bfloat16)
    value_grad = from_heads(value_parts).astype(jnp.bfloat16)
    return (query_grad, key_grad, value_grad, input_grad)
```

```python
import jax
import jax.numpy as jnp
from jax import lax
from jax.sharding import PartitionSpec as P

EPSILON = 1e-06
F32 = jnp.float32
BF16 = jnp.bfloat16


def mm(a, b):
    return jnp.dot(a, b, preferred_element_type=F32)


def mm_t(a, b):
    return lax.dot_general(a, b, (((1,), (1,)), ((), ())), preferred_element_type=F32)


def heads_dot(spec, a, b):
    return jnp.einsum(spec, a, b, preferred_element_type=F32)


def body(
    queries,
    key_rows,
    value_rows,
    decay_rates,
    w_out,
    inputs,
    cotangent,
    norm_gain,
    expert_ids,
    gate_weights,
    w_gate,
    w_up,
    w_down,
):
    length = queries.shape[0]
    head_count = decay_rates.shape[0]
    head_size = queries.shape[1] // head_count
    width = w_out.shape[1]
    half = width // 2
    tok_share = inputs.shape[0]
    pair_share = 2 * tok_share
    seq_count = lax.axis_size("seq")
    mp_count = lax.axis_size("mp")
    z_count = mp_count // 2
    seq_place = lax.axis_index("seq")
    core = lax.rem(lax.axis_index("mp"), 2)
    z_groups = [[2 * k + c for k in range(z_count)] for c in range(2)]
    core_groups = [[2 * k, 2 * k + 1] for k in range(z_count)]
    swap_pairs = [(i, i ^ 1) for i in range(mp_count)]

    def swap(x):
        return lax.ppermute(x, "mp", swap_pairs)

    def own_half(x, axis):
        return lax.dynamic_slice_in_dim(x, core * half, half, axis)

    def other_half(x, axis):
        return lax.dynamic_slice_in_dim(x, (1 - core) * half, half, axis)

    def by_core(mine, theirs, axis):
        return jnp.where(
            core == 0,
            jnp.concatenate([mine, theirs], axis=axis),
            jnp.concatenate([theirs, mine], axis=axis),
        )

    def spread_z(x):
        copies = jnp.broadcast_to(x[None], (z_count,) + x.shape)
        out = lax.all_to_all(copies, "mp", 0, 0, axis_index_groups=z_groups, tiled=True)
        return out.reshape((z_count * x.shape[0],) + x.shape[1:])

    def sum_z(x):
        parts = x.reshape(z_count, pair_share, half)
        out = lax.all_to_all(parts, "mp", 0, 0, axis_index_groups=z_groups, tiled=True)
        return jnp.sum(out.astype(F32), axis=0)

    def to_heads(matrix):
        return matrix.reshape(length, head_count, head_size).transpose(1, 0, 2)

    def from_heads(blocks):
        return blocks.transpose(1, 0, 2).reshape(length, head_count * head_size)

    cot_all = lax.all_gather(cotangent, ("seq", "mp"), axis=0, tiled=True)

    capacity = 4 * length // seq_count
    labels = jnp.arange(seq_count, dtype=jnp.int32)
    first_pick = expert_ids[:, 0:1] == labels[None, :]
    second_pick = expert_ids[:, 1:2] == labels[None, :]
    chosen = (first_pick | second_pick).astype(jnp.int32)
    weight = jnp.where(first_pick, gate_weights[:, 0:1], 0.0) + jnp.where(
        second_pick, gate_weights[:, 1:2], 0.0
    )
    ranking = jnp.cumsum(chosen, axis=0) - 1
    slot_ids = jnp.arange(capacity, dtype=jnp.int32)
    placed = (chosen.T[:, None, :] == 1) & (ranking.T[:, None, :] == slot_ids[None, :, None])
    token_places = jnp.arange(length, dtype=jnp.int32)
    slot_token = jnp.sum(jnp.where(placed, token_places[None, None, :], 0), axis=2)
    slot_weight = jnp.sum(jnp.where(placed, weight.T[:, None, :], 0.0), axis=2)
    placing = placed.astype(BF16).reshape(seq_count * capacity, length)
    weight_top = slot_weight.astype(BF16)
    weight_low = (slot_weight - weight_top.astype(F32)).astype(BF16)
    notes = jnp.stack([slot_token.astype(BF16), weight_top, weight_low], axis=1)
    notes = jnp.pad(notes, ((0, 0), (0, 13), (0, head_size - capacity)))

    both = jnp.concatenate([inputs, cotangent], axis=0)
    both_kept, both_got = own_half(both, 1), swap(other_half(both, 1))
    pair_inputs = by_core(both_kept[:tok_share], both_got[:tok_share], 0).astype(F32)
    pair_cot = by_core(both_kept[tok_share:], both_got[tok_share:], 0).astype(F32)
    gain = own_half(norm_gain, 0)[None, :]

    query_heads, key_heads, value_heads = map(to_heads, (queries, key_rows, value_rows))
    places = jnp.arange(length).astype(F32)
    offset = places[:, None] - places[None, :]
    causal = offset >= 0
    clipped = jnp.where(causal, offset, 0.0)
    decay_band = jnp.where(causal[None], jnp.exp(-decay_rates[:, None, None] * clipped[None]), 0.0)
    head_decay = jnp.exp(-decay_rates[:, None] * places[None, :])[:, :, None]
    tail_decay = jnp.exp(-decay_rates[:, None] * (length - 1.0 - places)[None, :])[:, :, None]
    step_decay = jnp.exp(-decay_rates)[:, None, None]

    def exchange_states(states, extra):
        sent = states.astype(BF16).reshape(head_count * head_size, head_size)
        sent = jnp.broadcast_to(sent[None], (seq_count,) + sent.shape)
        if extra is not None:
            sent = jnp.concatenate([sent, extra], axis=1)
        return lax.all_to_all(sent, "seq", 0, 0, tiled=True)

    def combine_states(states, ahead):
        rate = decay_rates[:, None] * length * jnp.maximum(ahead, 0).astype(F32)[None, :]
        share = jnp.where(ahead[None, :] >= 0, jnp.exp(-rate), 0.0)
        states = states.reshape(seq_count, head_count, head_size, head_size).astype(F32)
        return jnp.sum(share.T[:, :, None, None] * states, axis=0)

    peers = jnp.arange(seq_count, dtype=jnp.int32)
    local_state = heads_dot(
        "htd,hte->hde",
        (step_decay * tail_decay * key_heads.astype(F32)).astype(BF16),
        value_heads,
    )
    arrived = exchange_states(local_state, notes)
    entering = combine_states(arrived[:, : head_count * head_size], seq_place - 1 - peers)
    entering_b = entering.astype(BF16)
    arrived_notes = arrived[:, head_count * head_size :, :capacity]
    scores = heads_dot("htd,hsd->hts", query_heads, key_heads) * decay_band
    scores_b = scores.astype(BF16)
    attended = heads_dot("hts,hse->hte", scores_b, value_heads)
    attended = attended + head_decay * heads_dot("htd,hde->hte", query_heads, entering_b)
    attended_b = from_heads(attended).astype(BF16)

    out_own, out_other = own_half(w_out, 1), other_half(w_out, 1)
    got = swap(mm(attended_b, out_other).astype(BF16))
    chip_mixed = (mm(attended_b, out_own) + got.astype(F32)).astype(BF16)
    stream = pair_inputs + sum_z(chip_mixed)

    def over_features(x):
        total = jnp.sum(x, axis=1, keepdims=True)
        return lax.psum(total, "mp", axis_index_groups=core_groups) / width

    inverse = lax.rsqrt(over_features(stream * stream) + EPSILON)
    normed = stream * inverse
    expert_in = (normed * gain).astype(BF16)

    group_in = spread_z(expert_in)
    outgoing = mm(placing, group_in).astype(BF16).reshape(seq_count, capacity, half)
    rows_own = lax.all_to_all(outgoing, "seq", 0, 0, tiled=True).reshape(-1, half)
    rows_other = swap(rows_own)
    gate_own, gate_other = own_half(w_gate[0], 0), other_half(w_gate[0], 0)
    up_own, up_other = own_half(w_up[0], 0), other_half(w_up[0], 0)

    hidden_all = mm_t(cot_all, w_down[0]).reshape(seq_count, length, -1)
    note_token = arrived_notes[:, 0, :].astype(jnp.int32)
    note_weight = arrived_notes[:, 1, :].astype(F32) + arrived_notes[:, 2, :].astype(F32)
    taken = (note_token[:, :, None] == token_places[None, None, :]).astype(F32)
    hidden_grad = jnp.einsum("bkt,bth->bkh", taken, hidden_all, precision=lax.Precision.HIGHEST)
    hidden_grad = (hidden_grad * note_weight[:, :, None]).reshape(seq_count * capacity, -1)

    gate_pre = mm(rows_own, gate_own) + mm(rows_other, gate_other)
    up_pre = mm(rows_own, up_own) + mm(rows_other, up_other)
    sigma = jax.nn.sigmoid(gate_pre)
    gate_grad = (hidden_grad * up_pre * sigma * (1.0 + gate_pre * (1.0 - sigma))).astype(BF16)
    up_grad = (hidden_grad * gate_pre * sigma).astype(BF16)
    got = swap((mm_t(gate_grad, gate_other) + mm_t(up_grad, up_other)).astype(BF16))
    slots = mm_t(gate_grad, gate_own) + mm_t(up_grad, up_own) + got.astype(F32)
    slots = slots.astype(BF16).reshape(seq_count, capacity, half)

    returned = lax.all_to_all(slots, "seq", 0, 0, tiled=True).reshape(-1, half)
    token_part = lax.dot_general(
        placing, returned, (((0,), (0,)), ((), ())), preferred_element_type=F32
    )
    expert_grad = sum_z(token_part.astype(BF16))
    scaled = expert_grad * gain
    stream_grad = inverse * (scaled - normed * over_features(scaled * normed)) + pair_cot
    pair_grad = stream_grad.astype(BF16)

    pair_kept = lax.dynamic_slice_in_dim(pair_grad, core * tok_share, tok_share, 0)
    pair_sent = lax.dynamic_slice_in_dim(pair_grad, (1 - core) * tok_share, tok_share, 0)
    input_grad = by_core(pair_kept, swap(pair_sent), 1)

    block_own = spread_z(pair_grad)
    block_other = swap(block_own)
    attended_grad = mm_t(block_own, out_own) + mm_t(block_other, out_other)
    grad_heads = to_heads(attended_grad)
    grad_b = grad_heads.astype(BF16)
    local_adjoint = heads_dot(
        "htd,hte->hde",
        query_heads,
        (step_decay * head_decay * grad_heads).astype(BF16),
    )
    leaving = combine_states(exchange_states(local_adjoint, None), peers - 1 - seq_place)
    leaving_b = leaving.astype(BF16)
    grad_scores = (heads_dot("hte,hse->hts", grad_b, value_heads) * decay_band).astype(BF16)
    query_part = heads_dot("hts,hsd->htd", grad_scores, key_heads)
    query_part = query_part + head_decay * heads_dot("hte,hde->htd", grad_b, entering_b)
    key_part = heads_dot("hts,htd->hsd", grad_scores, query_heads)
    key_part = key_part + tail_decay * heads_dot("hse,hde->hsd", value_heads, leaving_b)
    value_part = heads_dot("hts,hte->hse", scores_b, grad_b)
    value_part = value_part + tail_decay * heads_dot("hsd,hde->hse", key_heads, leaving_b)
    query_grad = from_heads(query_part).astype(BF16)
    key_grad = from_heads(key_part).astype(BF16)
    value_grad = from_heads(value_part).astype(BF16)
    return (query_grad, key_grad, value_grad, input_grad)


def solution(mesh):
    placed = (
        P("seq", "mp"),
        P("seq", "mp"),
        P("seq", "mp"),
        P("mp"),
        P("mp", None),
        P(("seq", "mp"), None),
        P(("seq", "mp"), None),
        P(),
        P("seq", None),
        P("seq", None),
        P("seq", None, "mp"),
        P("seq", None, "mp"),
        P("seq", "mp", None),
    )
    return jax.shard_map(
        body,
        mesh=mesh,
        in_specs=placed,
        out_specs=(P("seq", "mp"), P("seq", "mp"), P("seq", "mp"), P(("seq", "mp"), None)),
        check_vma=False,
    )
```

```python
import jax
import jax.numpy as jnp
from jax import lax
from jax.sharding import PartitionSpec as P

EPSILON = 1e-06
F32 = jnp.float32
BF16 = jnp.bfloat16


def mm(a, b):
    return jnp.dot(a, b, preferred_element_type=F32)


def mm_t(a, b):
    return lax.dot_general(a, b, (((1,), (1,)), ((), ())), preferred_element_type=F32)


def heads_dot(spec, a, b):
    return jnp.einsum(spec, a, b, preferred_element_type=F32)


def body(
    queries,
    key_rows,
    value_rows,
    decay_rates,
    w_out,
    inputs,
    cotangent,
    norm_gain,
    expert_ids,
    gate_weights,
    w_gate,
    w_up,
    w_down,
):
    length = queries.shape[0]
    head_count = decay_rates.shape[0]
    head_size = queries.shape[1] // head_count
    width = w_out.shape[1]
    half = width // 2
    tok_share = inputs.shape[0]
    pair_share = 2 * tok_share
    seq_count = lax.axis_size("seq")
    mp_count = lax.axis_size("mp")
    z_count = mp_count // 2
    seq_place = lax.axis_index("seq")
    core = lax.rem(lax.axis_index("mp"), 2)
    z_groups = [[2 * k + c for k in range(z_count)] for c in range(2)]
    core_groups = [[2 * k, 2 * k + 1] for k in range(z_count)]
    swap_pairs = [(i, i ^ 1) for i in range(mp_count)]

    def swap(x):
        return lax.ppermute(x, "mp", swap_pairs)

    def own_half(x, axis):
        return lax.dynamic_slice_in_dim(x, core * half, half, axis)

    def other_half(x, axis):
        return lax.dynamic_slice_in_dim(x, (1 - core) * half, half, axis)

    def by_core(mine, theirs, axis):
        return jnp.where(
            core == 0,
            jnp.concatenate([mine, theirs], axis=axis),
            jnp.concatenate([theirs, mine], axis=axis),
        )

    def spread_z(x):
        copies = jnp.broadcast_to(x[None], (z_count,) + x.shape)
        out = lax.all_to_all(copies, "mp", 0, 0, axis_index_groups=z_groups, tiled=True)
        return out.reshape((z_count * x.shape[0],) + x.shape[1:])

    z_bits = z_count.bit_length() - 1

    def double_z(x, level):
        bit = 2 << (z_bits - 1 - level)
        theirs = lax.ppermute(x, "mp", [(i, i ^ bit) for i in range(mp_count)])
        upper = lax.rem(lax.axis_index("mp") // bit, 2) == 1
        first, second = jnp.where(upper, theirs, x), jnp.where(upper, x, theirs)
        return jnp.stack([first, second], axis=level)

    def sum_z(x):
        parts = x.reshape(z_count, pair_share, half)
        out = lax.all_to_all(parts, "mp", 0, 0, axis_index_groups=z_groups, tiled=True)
        return jnp.sum(out.astype(F32), axis=0)

    def to_heads(matrix):
        return matrix.reshape(length, head_count, head_size).transpose(1, 0, 2)

    def from_heads(blocks):
        return blocks.transpose(1, 0, 2).reshape(length, head_count * head_size)

    capacity = 4 * length // seq_count
    labels = jnp.arange(seq_count, dtype=jnp.int32)
    first_pick = expert_ids[:, 0:1] == labels[None, :]
    second_pick = expert_ids[:, 1:2] == labels[None, :]
    chosen = (first_pick | second_pick).astype(jnp.int32)
    weight = jnp.where(first_pick, gate_weights[:, 0:1], 0.0) + jnp.where(
        second_pick, gate_weights[:, 1:2], 0.0
    )
    ranking = jnp.cumsum(chosen, axis=0) - 1
    slot_ids = jnp.arange(capacity, dtype=jnp.int32)
    placed = (chosen.T[:, None, :] == 1) & (ranking.T[:, None, :] == slot_ids[None, :, None])
    placing = placed.astype(BF16).reshape(seq_count * capacity, length)
    slot_weight = jnp.sum(jnp.where(placed, weight.T[:, None, :], 0.0), axis=2)

    both = jnp.concatenate([inputs, cotangent], axis=0)
    both_kept, both_got = own_half(both, 1), swap(other_half(both, 1))
    pair_inputs = by_core(both_kept[:tok_share], both_got[:tok_share], 0).astype(F32)
    pair_cot_b = by_core(both_kept[tok_share:], both_got[tok_share:], 0)
    pair_cot = pair_cot_b.astype(F32)
    gain = own_half(norm_gain, 0)[None, :]

    query_heads, key_heads, value_heads = map(to_heads, (queries, key_rows, value_rows))
    places = jnp.arange(length).astype(F32)
    offset = places[:, None] - places[None, :]
    causal = offset >= 0
    clipped = jnp.where(causal, offset, 0.0)
    decay_band = jnp.where(causal[None], jnp.exp(-decay_rates[:, None, None] * clipped[None]), 0.0)
    head_decay = jnp.exp(-decay_rates[:, None] * places[None, :])[:, :, None]
    tail_decay = jnp.exp(-decay_rates[:, None] * (length - 1.0 - places)[None, :])[:, :, None]
    step_decay = jnp.exp(-decay_rates)[:, None, None]

    def exchange_states(states):
        sent = states.astype(BF16).reshape(head_count * head_size, head_size)
        sent = jnp.broadcast_to(sent[None], (seq_count,) + sent.shape)
        return lax.all_to_all(sent, "seq", 0, 0, tiled=True)

    def combine_states(states, ahead):
        rate = decay_rates[:, None] * length * jnp.maximum(ahead, 0).astype(F32)[None, :]
        share = jnp.where(ahead[None, :] >= 0, jnp.exp(-rate), 0.0)
        states = states.reshape(seq_count, head_count, head_size, head_size).astype(F32)
        return jnp.sum(share.T[:, :, None, None] * states, axis=0)

    peers = jnp.arange(seq_count, dtype=jnp.int32)
    local_state = heads_dot(
        "htd,hte->hde",
        (step_decay * tail_decay * key_heads.astype(F32)).astype(BF16),
        value_heads,
    )
    entering = combine_states(exchange_states(local_state), seq_place - 1 - peers)
    entering_b = entering.astype(BF16)
    scores = heads_dot("htd,hsd->hts", query_heads, key_heads) * decay_band
    scores_b = scores.astype(BF16)
    attended = heads_dot("hts,hse->hte", scores_b, value_heads)
    attended = attended + head_decay * heads_dot("htd,hde->hte", query_heads, entering_b)
    attended_b = from_heads(attended).astype(BF16)

    out_own, out_other = own_half(w_out, 1), other_half(w_out, 1)
    got = swap(mm(attended_b, out_other).astype(BF16))
    chip_mixed = (mm(attended_b, out_own) + got.astype(F32)).astype(BF16)
    block_cot = pair_cot_b
    for level in range(z_bits // 2):
        block_cot = double_z(block_cot, level)
    block_cot, chip_mixed = lax.optimization_barrier((block_cot, chip_mixed))
    for level in range(z_bits // 2, z_bits):
        block_cot = double_z(block_cot, level)
    block_cot = block_cot.reshape(length, half)
    stream = pair_inputs + sum_z(chip_mixed)

    def over_features(x):
        total = jnp.sum(x, axis=1, keepdims=True)
        return lax.psum(total, "mp", axis_index_groups=core_groups) / width

    inverse = lax.rsqrt(over_features(stream * stream) + EPSILON)
    normed = stream * inverse
    expert_in = (normed * gain).astype(BF16)
    block_cot, expert_in = lax.optimization_barrier((block_cot, expert_in))

    group_in = spread_z(expert_in)
    outgoing = mm(placing, group_in).astype(BF16).reshape(seq_count, capacity, half)
    weighted = (slot_weight.reshape(-1, 1) * mm(placing, block_cot)).astype(BF16)
    weighted = weighted.reshape(seq_count, capacity, half)
    cot_own = lax.all_to_all(weighted, "seq", 0, 0, tiled=True).reshape(-1, half)
    cot_own, outgoing = lax.optimization_barrier((cot_own, outgoing))
    cot_other = swap(cot_own)
    rows_own = lax.all_to_all(outgoing, "seq", 0, 0, tiled=True).reshape(-1, half)
    rows_other = swap(rows_own)
    gate_own, gate_other = own_half(w_gate[0], 0), other_half(w_gate[0], 0)
    up_own, up_other = own_half(w_up[0], 0), other_half(w_up[0], 0)

    down_own, down_other = own_half(w_down[0], 1), other_half(w_down[0], 1)
    hidden_grad = mm_t(cot_own, down_own) + mm_t(cot_other, down_other)
    gate_pre = mm(rows_own, gate_own) + mm(rows_other, gate_other)
    up_pre = mm(rows_own, up_own) + mm(rows_other, up_other)
    sigma = jax.nn.sigmoid(gate_pre)
    gate_grad = (hidden_grad * up_pre * sigma * (1.0 + gate_pre * (1.0 - sigma))).astype(BF16)
    up_grad = (hidden_grad * gate_pre * sigma).astype(BF16)
    got = swap((mm_t(gate_grad, gate_other) + mm_t(up_grad, up_other)).astype(BF16))
    slots = mm_t(gate_grad, gate_own) + mm_t(up_grad, up_own) + got.astype(F32)
    slots = slots.astype(BF16).reshape(seq_count, capacity, half)

    returned = lax.all_to_all(slots, "seq", 0, 0, tiled=True).reshape(-1, half)
    token_part = lax.dot_general(
        placing, returned, (((0,), (0,)), ((), ())), preferred_element_type=F32
    )
    expert_grad = sum_z(token_part.astype(BF16))
    scaled = expert_grad * gain
    stream_grad = inverse * (scaled - normed * over_features(scaled * normed)) + pair_cot
    pair_grad = stream_grad.astype(BF16)

    pair_kept = lax.dynamic_slice_in_dim(pair_grad, core * tok_share, tok_share, 0)
    pair_sent = lax.dynamic_slice_in_dim(pair_grad, (1 - core) * tok_share, tok_share, 0)
    input_grad = by_core(pair_kept, swap(pair_sent), 1)

    block_own = spread_z(pair_grad)
    block_other = swap(block_own)
    attended_grad = mm_t(block_own, out_own) + mm_t(block_other, out_other)
    grad_heads = to_heads(attended_grad)
    grad_b = grad_heads.astype(BF16)
    local_adjoint = heads_dot(
        "htd,hte->hde",
        query_heads,
        (step_decay * head_decay * grad_heads).astype(BF16),
    )
    leaving = combine_states(exchange_states(local_adjoint), peers - 1 - seq_place)
    leaving_b = leaving.astype(BF16)
    grad_scores = (heads_dot("hte,hse->hts", grad_b, value_heads) * decay_band).astype(BF16)
    query_part = heads_dot("hts,hsd->htd", grad_scores, key_heads)
    query_part = query_part + head_decay * heads_dot("hte,hde->htd", grad_b, entering_b)
    key_part = heads_dot("hts,htd->hsd", grad_scores, query_heads)
    key_part = key_part + tail_decay * heads_dot("hse,hde->hsd", value_heads, leaving_b)
    value_part = heads_dot("hts,hte->hse", scores_b, grad_b)
    value_part = value_part + tail_decay * heads_dot("hsd,hde->hse", key_heads, leaving_b)
    query_grad = from_heads(query_part).astype(BF16)
    key_grad = from_heads(key_part).astype(BF16)
    value_grad = from_heads(value_part).astype(BF16)
    return (query_grad, key_grad, value_grad, input_grad)


def solution(mesh):
    placed = (
        P("seq", "mp"),
        P("seq", "mp"),
        P("seq", "mp"),
        P("mp"),
        P("mp", None),
        P(("seq", "mp"), None),
        P(("seq", "mp"), None),
        P(),
        P("seq", None),
        P("seq", None),
        P("seq", None, "mp"),
        P("seq", None, "mp"),
        P("seq", "mp", None),
    )
    return jax.shard_map(
        body,
        mesh=mesh,
        in_specs=placed,
        out_specs=(P("seq", "mp"), P("seq", "mp"), P("seq", "mp"), P(("seq", "mp"), None)),
        check_vma=False,
    )
```

```python
import jax
import jax.numpy as jnp
from jax import lax
from jax.sharding import PartitionSpec as P

EPSILON = 1e-06
F32 = jnp.float32
BF16 = jnp.bfloat16


def mm(a, b):
    return jnp.dot(a, b, preferred_element_type=F32)


def mm_t(a, b):
    return lax.dot_general(a, b, (((1,), (1,)), ((), ())), preferred_element_type=F32)


def heads_dot(spec, a, b):
    return jnp.einsum(spec, a, b, preferred_element_type=F32)


def body(
    queries,
    key_rows,
    value_rows,
    decay_rates,
    w_out,
    inputs,
    cotangent,
    norm_gain,
    expert_ids,
    gate_weights,
    w_gate,
    w_up,
    w_down,
):
    length = queries.shape[0]
    head_count = decay_rates.shape[0]
    head_size = queries.shape[1] // head_count
    width = w_out.shape[1]
    half = width // 2
    tok_share = inputs.shape[0]
    pair_share = 2 * tok_share
    seq_count = lax.axis_size("seq")
    mp_count = lax.axis_size("mp")
    z_count = mp_count // 2
    seq_place = lax.axis_index("seq")
    core = lax.rem(lax.axis_index("mp"), 2)
    z_groups = [[2 * k + c for k in range(z_count)] for c in range(2)]
    core_groups = [[2 * k, 2 * k + 1] for k in range(z_count)]
    swap_pairs = [(i, i ^ 1) for i in range(mp_count)]

    def swap(x):
        return lax.ppermute(x, "mp", swap_pairs)

    def own_half(x, axis):
        return lax.dynamic_slice_in_dim(x, core * half, half, axis)

    def other_half(x, axis):
        return lax.dynamic_slice_in_dim(x, (1 - core) * half, half, axis)

    def by_core(mine, theirs, axis):
        return jnp.where(
            core == 0,
            jnp.concatenate([mine, theirs], axis=axis),
            jnp.concatenate([theirs, mine], axis=axis),
        )

    def spread_z(x):
        copies = jnp.broadcast_to(x[None], (z_count,) + x.shape)
        out = lax.all_to_all(copies, "mp", 0, 0, axis_index_groups=z_groups, tiled=True)
        return out.reshape((z_count * x.shape[0],) + x.shape[1:])

    z_odd = lax.rem(lax.axis_index("mp") // 2, 2)

    def own_quarter(x):
        return lax.dynamic_slice_in_dim(x, z_odd * (half // 2), half // 2, 1)

    def other_quarter(x):
        return lax.dynamic_slice_in_dim(x, (1 - z_odd) * (half // 2), half // 2, 1)

    def across_z(x, offset):
        return lax.ppermute(x, "mp", [(i, i ^ (2 * offset)) for i in range(mp_count)])

    def sum_z(x):
        parts = x.reshape(z_count, pair_share, half)
        out = lax.all_to_all(parts, "mp", 0, 0, axis_index_groups=z_groups, tiled=True)
        return jnp.sum(out.astype(F32), axis=0)

    def to_heads(matrix):
        return matrix.reshape(length, head_count, head_size).transpose(1, 0, 2)

    def from_heads(blocks):
        return blocks.transpose(1, 0, 2).reshape(length, head_count * head_size)

    capacity = 4 * length // seq_count
    labels = jnp.arange(seq_count, dtype=jnp.int32)
    first_pick = expert_ids[:, 0:1] == labels[None, :]
    second_pick = expert_ids[:, 1:2] == labels[None, :]
    chosen = (first_pick | second_pick).astype(jnp.int32)
    weight = jnp.where(first_pick, gate_weights[:, 0:1], 0.0) + jnp.where(
        second_pick, gate_weights[:, 1:2], 0.0
    )
    ranking = jnp.cumsum(chosen, axis=0) - 1
    slot_ids = jnp.arange(capacity, dtype=jnp.int32)
    placed = (chosen.T[:, None, :] == 1) & (ranking.T[:, None, :] == slot_ids[None, :, None])
    placing = placed.astype(BF16).reshape(seq_count * capacity, length)
    slot_weight = jnp.sum(jnp.where(placed, weight.T[:, None, :], 0.0), axis=2)

    query_heads, key_heads, value_heads = map(to_heads, (queries, key_rows, value_rows))
    places = jnp.arange(length).astype(F32)
    offset = places[:, None] - places[None, :]
    causal = offset >= 0
    clipped = jnp.where(causal, offset, 0.0)
    decay_band = jnp.where(causal[None], jnp.exp(-decay_rates[:, None, None] * clipped[None]), 0.0)
    head_decay = jnp.exp(-decay_rates[:, None] * places[None, :])[:, :, None]
    tail_decay = jnp.exp(-decay_rates[:, None] * (length - 1.0 - places)[None, :])[:, :, None]
    step_decay = jnp.exp(-decay_rates)[:, None, None]

    def exchange_states(states):
        sent = states.astype(BF16).reshape(head_count * head_size, head_size)
        sent = jnp.broadcast_to(sent[None], (seq_count,) + sent.shape)
        return lax.all_to_all(sent, "seq", 0, 0, tiled=True)

    def combine_states(states, ahead):
        rate = decay_rates[:, None] * length * jnp.maximum(ahead, 0).astype(F32)[None, :]
        share = jnp.where(ahead[None, :] >= 0, jnp.exp(-rate), 0.0)
        states = states.reshape(seq_count, head_count, head_size, head_size).astype(F32)
        return jnp.sum(share.T[:, :, None, None] * states, axis=0)

    peers = jnp.arange(seq_count, dtype=jnp.int32)
    local_state = heads_dot(
        "htd,hte->hde",
        (step_decay * tail_decay * key_heads.astype(F32)).astype(BF16),
        value_heads,
    )
    local_state = local_state.astype(BF16)

    both = jnp.concatenate([inputs, cotangent], axis=0)
    hidden_units = w_down.shape[1]
    both, gate_in, up_in, down_in, local_state = lax.optimization_barrier(
        (both, w_gate[0], w_up[0], w_down[0], local_state)
    )
    weights = jnp.concatenate([gate_in.T, up_in.T, down_in], axis=0)
    both_kept, both_got = own_half(both, 1), swap(other_half(both, 1))
    weights_kept, weights_got = lax.optimization_barrier(
        (own_half(weights, 1), swap(other_half(weights, 1)))
    )
    pair_inputs = by_core(both_kept[:tok_share], both_got[:tok_share], 0).astype(F32)
    pair_cot_b = by_core(both_kept[tok_share:], both_got[tok_share:], 0)
    pair_cot = pair_cot_b.astype(F32)
    gain = own_half(norm_gain, 0)[None, :]

    entering = combine_states(exchange_states(local_state), seq_place - 1 - peers)
    entering_b = entering.astype(BF16)
    scores = heads_dot("htd,hsd->hts", query_heads, key_heads) * decay_band
    scores_b = scores.astype(BF16)
    attended = heads_dot("hts,hse->hte", scores_b, value_heads)
    attended = attended + head_decay * heads_dot("htd,hde->hte", query_heads, entering_b)
    attended_b = from_heads(attended).astype(BF16)

    out_own, out_other = own_half(w_out, 1), other_half(w_out, 1)
    got = swap(mm(attended_b, out_other).astype(BF16))
    chip_mixed = (mm(attended_b, out_own) + got.astype(F32)).astype(BF16)
    quarters = pair_cot_b.reshape(pair_share, 2, half // 2).transpose(1, 0, 2)
    quarters = jnp.broadcast_to(quarters[None], (z_count // 2,) + quarters.shape)
    sent = jnp.concatenate(
        [
            chip_mixed.reshape(z_count, pair_share, half),
            quarters.reshape(z_count, pair_share, half // 2),
        ],
        axis=2,
    )
    arrived = lax.all_to_all(sent, "mp", 0, 0, axis_index_groups=z_groups, tiled=True)
    stream = pair_inputs + jnp.sum(arrived[:, :, :half].astype(F32), axis=0)
    block_cot = arrived[:, :, half:].reshape(length, half // 2)

    def over_features(x):
        total = jnp.sum(x, axis=1, keepdims=True)
        return lax.psum(total, "mp", axis_index_groups=core_groups) / width

    inverse = lax.rsqrt(over_features(stream * stream) + EPSILON)
    normed = stream * inverse
    expert_in = (normed * gain).astype(BF16)


    group_in = spread_z(expert_in)
    outgoing = mm(placing, group_in).astype(BF16).reshape(seq_count, capacity, half)
    weighted = (slot_weight.reshape(-1, 1) * mm(placing, block_cot)).astype(BF16)
    cot_own = lax.all_to_all(
        weighted.reshape(seq_count, capacity, half // 2), "seq", 0, 0, tiled=True
    ).reshape(-1, half // 2)
    cot_own, outgoing = lax.optimization_barrier((cot_own, outgoing))
    cot_pair = across_z(cot_own, 1)
    rows = lax.all_to_all(outgoing, "seq", 0, 0, tiled=True).reshape(-1, half)

    def features_part(part):
        pre = mm_t(part[: 2 * hidden_units], rows)
        down = part[2 * hidden_units :]
        hidden = mm_t(own_quarter(down), cot_own) + mm_t(other_quarter(down), cot_pair)
        return jnp.concatenate([pre, hidden], axis=0)

    got = swap(features_part(weights_got))
    pre = features_part(weights_kept) + got
    gate_pre, up_pre = pre[:hidden_units], pre[hidden_units : 2 * hidden_units]
    hidden_grad = pre[2 * hidden_units :]
    sigma = jax.nn.sigmoid(gate_pre)
    gate_grad = (hidden_grad * up_pre * sigma * (1.0 + gate_pre * (1.0 - sigma))).astype(BF16)
    up_grad = (hidden_grad * gate_pre * sigma).astype(BF16)
    grads = jnp.concatenate([gate_grad, up_grad], axis=0)
    grads_got = swap(grads)

    def units_part(units, part):
        return lax.dot_general(
            units, part, (((0,), (0,)), ((), ())), preferred_element_type=F32
        )

    slots = units_part(grads, weights_kept[: 2 * hidden_units])
    slots = slots + units_part(grads_got, weights_got[: 2 * hidden_units])
    slots = slots.astype(BF16).reshape(seq_count, capacity, half)

    returned = lax.all_to_all(slots, "seq", 0, 0, tiled=True).reshape(-1, half)
    token_part = lax.dot_general(
        placing, returned, (((0,), (0,)), ((), ())), preferred_element_type=F32
    )
    expert_grad = sum_z(token_part.astype(BF16))
    scaled = expert_grad * gain
    stream_grad = inverse * (scaled - normed * over_features(scaled * normed)) + pair_cot
    pair_grad = stream_grad.astype(BF16)

    block_own = spread_z(pair_grad)
    block_other = swap(block_own)
    attended_grad = mm_t(block_own, out_own) + mm_t(block_other, out_other)
    grad_heads = to_heads(attended_grad)
    grad_b = grad_heads.astype(BF16)
    local_adjoint = heads_dot(
        "htd,hte->hde",
        query_heads,
        (step_decay * head_decay * grad_heads).astype(BF16),
    )
    leaving = combine_states(exchange_states(local_adjoint), peers - 1 - seq_place)
    leaving_b = leaving.astype(BF16)
    grad_scores = (heads_dot("hte,hse->hts", grad_b, value_heads) * decay_band).astype(BF16)
    query_part = heads_dot("hts,hsd->htd", grad_scores, key_heads)
    query_part = query_part + head_decay * heads_dot("hte,hde->htd", grad_b, entering_b)
    key_part = heads_dot("hts,htd->hsd", grad_scores, query_heads)
    key_part = key_part + tail_decay * heads_dot("hse,hde->hsd", value_heads, leaving_b)
    value_part = heads_dot("hts,hte->hse", scores_b, grad_b)
    value_part = value_part + tail_decay * heads_dot("hsd,hde->hse", key_heads, leaving_b)
    query_grad = from_heads(query_part).astype(BF16)
    key_grad = from_heads(key_part).astype(BF16)
    value_grad = from_heads(value_part).astype(BF16)
    def own_tokens(x):
        return lax.dynamic_slice_in_dim(x, lax.axis_index("mp") * tok_share, tok_share, 0)

    input_grad = by_core(own_tokens(block_own), own_tokens(block_other), 1)
    return (query_grad, key_grad, value_grad, input_grad)


def solution(mesh):
    placed = (
        P("seq", "mp"),
        P("seq", "mp"),
        P("seq", "mp"),
        P("mp"),
        P("mp", None),
        P(("seq", "mp"), None),
        P(("seq", "mp"), None),
        P(),
        P("seq", None),
        P("seq", None),
        P("seq", None, "mp"),
        P("seq", None, "mp"),
        P("seq", "mp", None),
    )
    return jax.shard_map(
        body,
        mesh=mesh,
        in_specs=placed,
        out_specs=(P("seq", "mp"), P("seq", "mp"), P("seq", "mp"), P(("seq", "mp"), None)),
        check_vma=False,
    )
```

```python
import jax
import jax.numpy as jnp
from jax import lax
from jax.experimental import pallas as pl
from jax.experimental.pallas import tpu as pltpu
from jax.sharding import PartitionSpec as P

EPSILON = 1e-06
F32 = jnp.float32
BF16 = jnp.bfloat16


def mm(a, b):
    return jnp.dot(a, b, preferred_element_type=F32)


def mm_t(a, b):
    return lax.dot_general(a, b, (((1,), (1,)), ((), ())), preferred_element_type=F32)


def heads_dot(spec, a, b):
    return jnp.einsum(spec, a, b, preferred_element_type=F32)


LIMITS = pltpu.CompilerParams(vmem_limit_bytes=8 * 2**20)
VMEM = pl.BlockSpec(memory_space=pltpu.VMEM)
SMEM = pl.BlockSpec(memory_space=pltpu.SMEM)


def rows_of(length, lanes):
    return lax.broadcasted_iota(jnp.int32, (length, lanes), 0).astype(F32)


def state_kernel(head_size, first_power, step, rate_ref, left_ref, right_ref, out_ref):
    length = left_ref.shape[0]
    for head in range(rate_ref.shape[0]):
        columns = pl.ds(head * head_size, head_size)
        powers = first_power + step * rows_of(length, head_size)
        left = jnp.exp(-rate_ref[head] * powers) * left_ref[:, columns].astype(F32)
        state = lax.dot_general(
            left.astype(BF16),
            right_ref[:, columns].astype(BF16),
            (((0,), (0,)), ((), ())),
            preferred_element_type=F32,
        ).astype(BF16)
        for copy in range(out_ref.shape[0]):
            out_ref[copy, columns, :] = state


def state_copies(rates, left, right, copies, first_power, step):
    length, width = left.shape
    head_size = width // rates.shape[0]
    return pl.pallas_call(
        lambda *refs: state_kernel(head_size, first_power, step, *refs),
        out_shape=jax.ShapeDtypeStruct((copies, width, head_size), BF16),
        in_specs=[SMEM, VMEM, VMEM],
        out_specs=VMEM,
        cost_estimate=pl.CostEstimate(
            flops=2 * length * width * head_size,
            bytes_accessed=2 * (copies * width * head_size + 2 * length * width),
            transcendentals=length * width,
        ),
    )(rates, left, right)


def last_kernel(
    rate_ref, place_ref, states_ref, key_ref, value_ref, key_in_ref, value_in_ref, key_ref_out, value_ref_out
):
    length, width = key_ref.shape
    peers, _, head_size = states_ref.shape
    for head in range(rate_ref.shape[0]):
        rate = rate_ref[head]
        columns = pl.ds(head * head_size, head_size)
        leaving = jnp.zeros((head_size, head_size), F32)
        for peer in range(peers):
            ahead = peer - 1 - place_ref[0]
            power = jnp.full((1, head_size), rate * length * jnp.maximum(ahead, 0).astype(F32))
            share = jnp.where(ahead >= 0, jnp.exp(-power), 0.0)
            leaving = leaving + share * states_ref[peer, columns, :].astype(F32)
        leaving = leaving.astype(BF16)
        tail = jnp.exp(-rate * (length - 1.0 - rows_of(length, head_size)))
        key_part = key_in_ref[:, columns] + tail * mm_t(value_ref[:, columns], leaving)
        value_part = value_in_ref[:, columns] + tail * mm(key_ref[:, columns], leaving)
        key_ref_out[:, columns] = key_part.astype(BF16)
        value_ref_out[:, columns] = value_part.astype(BF16)


def last_grads(rates, place, states, key_rows, value_rows, key_inside, value_inside):
    length, width = key_rows.shape
    out = jax.ShapeDtypeStruct((length, width), BF16)
    return pl.pallas_call(
        last_kernel,
        out_shape=(out, out),
        in_specs=[SMEM, SMEM, VMEM, VMEM, VMEM, VMEM, VMEM],
        out_specs=(VMEM, VMEM),
        compiler_params=LIMITS,
        cost_estimate=pl.CostEstimate(
            flops=4 * length * width * states.shape[2],
            bytes_accessed=2 * states.size + 16 * length * width,
            transcendentals=length * width,
        ),
    )(rates, place.reshape(1), states, key_rows, value_rows, key_inside, value_inside)


def body(
    queries,
    key_rows,
    value_rows,
    decay_rates,
    w_out,
    inputs,
    cotangent,
    norm_gain,
    expert_ids,
    gate_weights,
    w_gate,
    w_up,
    w_down,
):
    length = queries.shape[0]
    head_count = decay_rates.shape[0]
    head_size = queries.shape[1] // head_count
    width = w_out.shape[1]
    half = width // 2
    tok_share = inputs.shape[0]
    pair_share = 2 * tok_share
    seq_count = lax.axis_size("seq")
    mp_count = lax.axis_size("mp")
    z_count = mp_count // 2
    seq_place = lax.axis_index("seq")
    core = lax.rem(lax.axis_index("mp"), 2)
    z_groups = [[2 * k + c for k in range(z_count)] for c in range(2)]
    core_groups = [[2 * k, 2 * k + 1] for k in range(z_count)]
    swap_pairs = [(i, i ^ 1) for i in range(mp_count)]

    def swap(x):
        return lax.ppermute(x, "mp", swap_pairs)

    def own_half(x, axis):
        return lax.dynamic_slice_in_dim(x, core * half, half, axis)

    def other_half(x, axis):
        return lax.dynamic_slice_in_dim(x, (1 - core) * half, half, axis)

    def by_core(mine, theirs, axis):
        return jnp.where(
            core == 0,
            jnp.concatenate([mine, theirs], axis=axis),
            jnp.concatenate([theirs, mine], axis=axis),
        )

    def spread_z(x):
        copies = jnp.broadcast_to(x[None], (z_count,) + x.shape)
        out = lax.all_to_all(copies, "mp", 0, 0, axis_index_groups=z_groups, tiled=True)
        return out.reshape((z_count * x.shape[0],) + x.shape[1:])

    z_odd = lax.rem(lax.axis_index("mp") // 2, 2)

    def own_quarter(x):
        return lax.dynamic_slice_in_dim(x, z_odd * (half // 2), half // 2, 1)

    def other_quarter(x):
        return lax.dynamic_slice_in_dim(x, (1 - z_odd) * (half // 2), half // 2, 1)

    def across_z(x, offset):
        return lax.ppermute(x, "mp", [(i, i ^ (2 * offset)) for i in range(mp_count)])

    def sum_z(x):
        parts = x.reshape(z_count, pair_share, half)
        out = lax.all_to_all(parts, "mp", 0, 0, axis_index_groups=z_groups, tiled=True)
        return jnp.sum(out.astype(F32), axis=0)

    def to_heads(matrix):
        return matrix.reshape(length, head_count, head_size).transpose(1, 0, 2)

    def from_heads(blocks):
        return blocks.transpose(1, 0, 2).reshape(length, head_count * head_size)

    capacity = 4 * length // seq_count
    labels = jnp.arange(seq_count, dtype=jnp.int32)
    first_pick = expert_ids[:, 0:1] == labels[None, :]
    second_pick = expert_ids[:, 1:2] == labels[None, :]
    chosen = (first_pick | second_pick).astype(jnp.int32)
    weight = jnp.where(first_pick, gate_weights[:, 0:1], 0.0) + jnp.where(
        second_pick, gate_weights[:, 1:2], 0.0
    )
    ranking = jnp.cumsum(chosen, axis=0) - 1
    slot_ids = jnp.arange(capacity, dtype=jnp.int32)
    placed = (chosen.T[:, None, :] == 1) & (ranking.T[:, None, :] == slot_ids[None, :, None])
    placing = placed.astype(BF16).reshape(seq_count * capacity, length)
    slot_weight = jnp.sum(jnp.where(placed, weight.T[:, None, :], 0.0), axis=2)

    query_heads, key_heads, value_heads = map(to_heads, (queries, key_rows, value_rows))
    places = jnp.arange(length).astype(F32)
    offset = places[:, None] - places[None, :]
    causal = offset >= 0
    clipped = jnp.where(causal, offset, 0.0)
    decay_band = jnp.where(causal[None], jnp.exp(-decay_rates[:, None, None] * clipped[None]), 0.0)
    head_decay = jnp.exp(-decay_rates[:, None] * places[None, :])[:, :, None]

    def exchange_states(sent):
        return lax.all_to_all(sent, "seq", 0, 0, tiled=True)

    def combine_states(states, ahead):
        rate = decay_rates[:, None] * length * jnp.maximum(ahead, 0).astype(F32)[None, :]
        share = jnp.where(ahead[None, :] >= 0, jnp.exp(-rate), 0.0)
        states = states.reshape(seq_count, head_count, head_size, head_size).astype(F32)
        return jnp.sum(share.T[:, :, None, None] * states, axis=0)

    peers = jnp.arange(seq_count, dtype=jnp.int32)
    local_state = state_copies(
        decay_rates, key_rows, value_rows, seq_count, float(length), -1.0
    )

    both = jnp.concatenate([inputs, cotangent], axis=0)
    hidden_units = w_down.shape[1]
    both, gate_in, up_in, down_in, local_state = lax.optimization_barrier(
        (both, w_gate[0], w_up[0], w_down[0], local_state)
    )
    weights = jnp.concatenate([gate_in.T, up_in.T, down_in], axis=0)
    both_kept, both_got = own_half(both, 1), swap(other_half(both, 1))
    weights_kept, weights_got = lax.optimization_barrier(
        (own_half(weights, 1), swap(other_half(weights, 1)))
    )
    pair_inputs = by_core(both_kept[:tok_share], both_got[:tok_share], 0).astype(F32)
    pair_cot_b = by_core(both_kept[tok_share:], both_got[tok_share:], 0)
    pair_cot = pair_cot_b.astype(F32)
    gain = own_half(norm_gain, 0)[None, :]

    entering = combine_states(exchange_states(local_state), seq_place - 1 - peers)
    entering_b = entering.astype(BF16)
    scores = heads_dot("htd,hsd->hts", query_heads, key_heads) * decay_band
    scores_b = scores.astype(BF16)
    attended = heads_dot("hts,hse->hte", scores_b, value_heads)
    attended = attended + head_decay * heads_dot("htd,hde->hte", query_heads, entering_b)
    attended_b = from_heads(attended).astype(BF16)

    out_own, out_other = own_half(w_out, 1), other_half(w_out, 1)
    got = swap(mm(attended_b, out_other).astype(BF16))
    chip_mixed = (mm(attended_b, out_own) + got.astype(F32)).astype(BF16)
    quarters = pair_cot_b.reshape(pair_share, 2, half // 2).transpose(1, 0, 2)
    quarters = jnp.broadcast_to(quarters[None], (z_count // 2,) + quarters.shape)
    sent = jnp.concatenate(
        [
            chip_mixed.reshape(z_count, pair_share, half),
            quarters.reshape(z_count, pair_share, half // 2),
        ],
        axis=2,
    )
    arrived = lax.all_to_all(sent, "mp", 0, 0, axis_index_groups=z_groups, tiled=True)
    stream = pair_inputs + jnp.sum(arrived[:, :, :half].astype(F32), axis=0)
    block_cot = arrived[:, :, half:].reshape(length, half // 2)

    def over_features(x):
        total = jnp.sum(x, axis=1, keepdims=True)
        return lax.psum(total, "mp", axis_index_groups=core_groups) / width

    inverse = lax.rsqrt(over_features(stream * stream) + EPSILON)
    normed = stream * inverse
    expert_in = (normed * gain).astype(BF16)


    group_in = spread_z(expert_in)
    outgoing = mm(placing, group_in).astype(BF16).reshape(seq_count, capacity, half)
    weighted = (slot_weight.reshape(-1, 1) * mm(placing, block_cot)).astype(BF16)
    cot_own = lax.all_to_all(
        weighted.reshape(seq_count, capacity, half // 2), "seq", 0, 0, tiled=True
    ).reshape(-1, half // 2)
    cot_own, outgoing = lax.optimization_barrier((cot_own, outgoing))
    cot_pair = across_z(cot_own, 1)
    rows = lax.all_to_all(outgoing, "seq", 0, 0, tiled=True).reshape(-1, half)

    def features_part(part):
        pre = mm_t(part[: 2 * hidden_units], rows)
        down = part[2 * hidden_units :]
        hidden = mm_t(own_quarter(down), cot_own) + mm_t(other_quarter(down), cot_pair)
        return jnp.concatenate([pre, hidden], axis=0)

    got = swap(features_part(weights_got))
    pre = features_part(weights_kept) + got
    gate_pre, up_pre = pre[:hidden_units], pre[hidden_units : 2 * hidden_units]
    hidden_grad = pre[2 * hidden_units :]
    sigma = jax.nn.sigmoid(gate_pre)
    gate_grad = (hidden_grad * up_pre * sigma * (1.0 + gate_pre * (1.0 - sigma))).astype(BF16)
    up_grad = (hidden_grad * gate_pre * sigma).astype(BF16)
    grads = jnp.concatenate([gate_grad, up_grad], axis=0)
    grads_got = swap(grads)

    def units_part(units, part):
        return lax.dot_general(
            units, part, (((0,), (0,)), ((), ())), preferred_element_type=F32
        )

    slots = units_part(grads, weights_kept[: 2 * hidden_units])
    slots = slots + units_part(grads_got, weights_got[: 2 * hidden_units])
    slots = slots.astype(BF16).reshape(seq_count, capacity, half)

    returned = lax.all_to_all(slots, "seq", 0, 0, tiled=True).reshape(-1, half)
    token_part = lax.dot_general(
        placing, returned, (((0,), (0,)), ((), ())), preferred_element_type=F32
    )
    expert_grad = sum_z(token_part.astype(BF16))
    scaled = expert_grad * gain
    stream_grad = inverse * (scaled - normed * over_features(scaled * normed)) + pair_cot
    pair_grad = stream_grad.astype(BF16)

    block_own = spread_z(pair_grad)
    block_other = swap(block_own)
    attended_grad = mm_t(block_own, out_own) + mm_t(block_other, out_other)
    grad_heads = to_heads(attended_grad)
    grad_b = grad_heads.astype(BF16)
    local_adjoint = heads_dot(
        "htd,hte->hde",
        query_heads,
        (jnp.exp(-decay_rates[:, None] * (places + 1.0)[None, :])[:, :, None] * grad_heads).astype(BF16),
    ).astype(BF16)
    local_adjoint = local_adjoint.reshape(head_count * head_size, head_size)
    local_adjoint = jnp.broadcast_to(local_adjoint[None], (seq_count,) + local_adjoint.shape)
    adjoints = exchange_states(local_adjoint)
    grad_scores = (heads_dot("hte,hse->hts", grad_b, value_heads) * decay_band).astype(BF16)
    query_part = heads_dot("hts,hsd->htd", grad_scores, key_heads)
    query_part = query_part + head_decay * heads_dot("hte,hde->htd", grad_b, entering_b)
    key_part = heads_dot("hts,htd->hsd", grad_scores, query_heads)
    value_part = heads_dot("hts,hte->hse", scores_b, grad_b)
    query_grad = from_heads(query_part).astype(BF16)
    key_grad, value_grad = last_grads(
        decay_rates,
        seq_place,
        adjoints,
        key_rows,
        value_rows,
        from_heads(key_part),
        from_heads(value_part),
    )

    def own_tokens(x):
        return lax.dynamic_slice_in_dim(x, lax.axis_index("mp") * tok_share, tok_share, 0)

    input_grad = by_core(own_tokens(block_own), own_tokens(block_other), 1)
    return (query_grad, key_grad, value_grad, input_grad)


def solution(mesh):
    placed = (
        P("seq", "mp"),
        P("seq", "mp"),
        P("seq", "mp"),
        P("mp"),
        P("mp", None),
        P(("seq", "mp"), None),
        P(("seq", "mp"), None),
        P(),
        P("seq", None),
        P("seq", None),
        P("seq", None, "mp"),
        P("seq", None, "mp"),
        P("seq", "mp", None),
    )
    return jax.shard_map(
        body,
        mesh=mesh,
        in_specs=placed,
        out_specs=(P("seq", "mp"), P("seq", "mp"), P("seq", "mp"), P(("seq", "mp"), None)),
        check_vma=False,
    )
```

```python
import jax
import jax.numpy as jnp
from jax import lax
from jax.experimental import pallas as pl
from jax.experimental.pallas import tpu as pltpu
from jax.sharding import PartitionSpec as P

EPSILON = 1e-06
F32 = jnp.float32
BF16 = jnp.bfloat16


def mm(a, b):
    return jnp.dot(a, b, preferred_element_type=F32)


def mm_t(a, b):
    return lax.dot_general(a, b, (((1,), (1,)), ((), ())), preferred_element_type=F32)


def heads_dot(spec, a, b):
    return jnp.einsum(spec, a, b, preferred_element_type=F32)


LIMITS = pltpu.CompilerParams(vmem_limit_bytes=8 * 2**20)
VMEM = pl.BlockSpec(memory_space=pltpu.VMEM)
SMEM = pl.BlockSpec(memory_space=pltpu.SMEM)


def rows_of(length, lanes):
    return lax.broadcasted_iota(jnp.int32, (length, lanes), 0).astype(F32)


def state_kernel(head_size, first_power, step, rate_ref, left_ref, right_ref, out_ref):
    length = left_ref.shape[0]
    for head in range(rate_ref.shape[0]):
        columns = pl.ds(head * head_size, head_size)
        powers = first_power + step * rows_of(length, head_size)
        left = jnp.exp(-rate_ref[head] * powers) * left_ref[:, columns].astype(F32)
        state = lax.dot_general(
            left.astype(BF16),
            right_ref[:, columns].astype(BF16),
            (((0,), (0,)), ((), ())),
            preferred_element_type=F32,
        ).astype(BF16)
        for copy in range(out_ref.shape[0]):
            out_ref[copy, columns, :] = state


def state_copies(rates, left, right, copies, first_power, step):
    length, width = left.shape
    head_size = width // rates.shape[0]
    return pl.pallas_call(
        lambda *refs: state_kernel(head_size, first_power, step, *refs),
        out_shape=jax.ShapeDtypeStruct((copies, width, head_size), BF16),
        in_specs=[SMEM, VMEM, VMEM],
        out_specs=VMEM,
        cost_estimate=pl.CostEstimate(
            flops=2 * length * width * head_size,
            bytes_accessed=2 * (copies * width * head_size + 2 * length * width),
            transcendentals=length * width,
        ),
    )(rates, left, right)


def last_kernel(
    rate_ref, place_ref, states_ref, key_ref, value_ref, key_in_ref, value_in_ref, key_ref_out, value_ref_out
):
    length, width = key_ref.shape
    peers, _, head_size = states_ref.shape
    for head in range(rate_ref.shape[0]):
        rate = rate_ref[head]
        columns = pl.ds(head * head_size, head_size)
        leaving = jnp.zeros((head_size, head_size), F32)
        for peer in range(peers):
            ahead = peer - 1 - place_ref[0]
            power = jnp.full((1, head_size), rate * length * jnp.maximum(ahead, 0).astype(F32))
            share = jnp.where(ahead >= 0, jnp.exp(-power), 0.0)
            leaving = leaving + share * states_ref[peer, columns, :].astype(F32)
        leaving = leaving.astype(BF16)
        tail = jnp.exp(-rate * (length - 1.0 - rows_of(length, head_size)))
        key_part = key_in_ref[:, columns] + tail * mm_t(value_ref[:, columns], leaving)
        value_part = value_in_ref[:, columns] + tail * mm(key_ref[:, columns], leaving)
        key_ref_out[:, columns] = key_part.astype(BF16)
        value_ref_out[:, columns] = value_part.astype(BF16)


def last_grads(rates, place, states, key_rows, value_rows, key_inside, value_inside):
    length, width = key_rows.shape
    out = jax.ShapeDtypeStruct((length, width), BF16)
    return pl.pallas_call(
        last_kernel,
        out_shape=(out, out),
        in_specs=[SMEM, SMEM, VMEM, VMEM, VMEM, VMEM, VMEM],
        out_specs=(VMEM, VMEM),
        compiler_params=LIMITS,
        cost_estimate=pl.CostEstimate(
            flops=4 * length * width * states.shape[2],
            bytes_accessed=2 * states.size + 16 * length * width,
            transcendentals=length * width,
        ),
    )(rates, place.reshape(1), states, key_rows, value_rows, key_inside, value_inside)


def body(
    queries,
    key_rows,
    value_rows,
    decay_rates,
    w_out,
    inputs,
    cotangent,
    norm_gain,
    expert_ids,
    gate_weights,
    w_gate,
    w_up,
    w_down,
):
    length = queries.shape[0]
    head_count = decay_rates.shape[0]
    head_size = queries.shape[1] // head_count
    width = w_out.shape[1]
    half = width // 2
    tok_share = inputs.shape[0]
    pair_share = 2 * tok_share
    seq_count = lax.axis_size("seq")
    mp_count = lax.axis_size("mp")
    z_count = mp_count // 2
    seq_place = lax.axis_index("seq")
    core = lax.rem(lax.axis_index("mp"), 2)
    z_groups = [[2 * k + c for k in range(z_count)] for c in range(2)]
    core_groups = [[2 * k, 2 * k + 1] for k in range(z_count)]
    swap_pairs = [(i, i ^ 1) for i in range(mp_count)]

    def swap(x):
        return lax.ppermute(x, "mp", swap_pairs)

    def own_half(x, axis):
        return lax.dynamic_slice_in_dim(x, core * half, half, axis)

    def other_half(x, axis):
        return lax.dynamic_slice_in_dim(x, (1 - core) * half, half, axis)

    def by_core(mine, theirs, axis):
        return jnp.where(
            core == 0,
            jnp.concatenate([mine, theirs], axis=axis),
            jnp.concatenate([theirs, mine], axis=axis),
        )

    def spread_z(x):
        copies = jnp.broadcast_to(x[None], (z_count,) + x.shape)
        out = lax.all_to_all(copies, "mp", 0, 0, axis_index_groups=z_groups, tiled=True)
        return out.reshape((z_count * x.shape[0],) + x.shape[1:])

    z_odd = lax.rem(lax.axis_index("mp") // 2, 2)

    def own_quarter(x):
        return lax.dynamic_slice_in_dim(x, z_odd * (half // 2), half // 2, 1)

    def other_quarter(x):
        return lax.dynamic_slice_in_dim(x, (1 - z_odd) * (half // 2), half // 2, 1)

    def across_z(x, offset):
        return lax.ppermute(x, "mp", [(i, i ^ (2 * offset)) for i in range(mp_count)])

    def sum_z(x):
        parts = x.reshape(z_count, pair_share, half)
        out = lax.all_to_all(parts, "mp", 0, 0, axis_index_groups=z_groups, tiled=True)
        return jnp.sum(out.astype(F32), axis=0)

    def to_heads(matrix):
        return matrix.reshape(length, head_count, head_size).transpose(1, 0, 2)

    def from_heads(blocks):
        return blocks.transpose(1, 0, 2).reshape(length, head_count * head_size)

    capacity = 4 * length // seq_count
    labels = jnp.arange(seq_count, dtype=jnp.int32)
    first_pick = expert_ids[:, 0:1] == labels[None, :]
    second_pick = expert_ids[:, 1:2] == labels[None, :]
    chosen = (first_pick | second_pick).astype(jnp.int32)
    weight = jnp.where(first_pick, gate_weights[:, 0:1], 0.0) + jnp.where(
        second_pick, gate_weights[:, 1:2], 0.0
    )
    ranking = jnp.cumsum(chosen, axis=0) - 1
    slot_ids = jnp.arange(capacity, dtype=jnp.int32)
    placed = (chosen.T[:, None, :] == 1) & (ranking.T[:, None, :] == slot_ids[None, :, None])
    placing = placed.astype(BF16).reshape(seq_count * capacity, length)
    slot_weight = jnp.sum(jnp.where(placed, weight.T[:, None, :], 0.0), axis=2)

    query_heads, key_heads, value_heads = map(to_heads, (queries, key_rows, value_rows))
    places = jnp.arange(length).astype(F32)
    offset = places[:, None] - places[None, :]
    causal = offset >= 0
    clipped = jnp.where(causal, offset, 0.0)
    decay_band = jnp.where(causal[None], jnp.exp(-decay_rates[:, None, None] * clipped[None]), 0.0)
    head_decay = jnp.exp(-decay_rates[:, None] * places[None, :])[:, :, None]

    def exchange_states(sent):
        return lax.all_to_all(sent, "seq", 0, 0, tiled=True)

    def combine_states(states, ahead):
        rate = decay_rates[:, None] * length * jnp.maximum(ahead, 0).astype(F32)[None, :]
        share = jnp.where(ahead[None, :] >= 0, jnp.exp(-rate), 0.0)
        states = states.reshape(seq_count, head_count, head_size, head_size).astype(F32)
        return jnp.sum(share.T[:, :, None, None] * states, axis=0)

    peers = jnp.arange(seq_count, dtype=jnp.int32)
    local_state = state_copies(
        decay_rates, key_rows, value_rows, seq_count, float(length), -1.0
    )

    both = jnp.concatenate([inputs, cotangent], axis=0)
    hidden_units = w_down.shape[1]
    both, gate_in, up_in, down_in, local_state = lax.optimization_barrier(
        (both, w_gate[0], w_up[0], w_down[0], local_state)
    )
    weights = jnp.concatenate([gate_in.T, up_in.T, down_in], axis=0)
    both_kept, both_got = own_half(both, 1), swap(other_half(both, 1))
    weights_kept, weights_got = lax.optimization_barrier(
        (own_half(weights, 1), swap(other_half(weights, 1)))
    )
    pair_inputs = by_core(both_kept[:tok_share], both_got[:tok_share], 0).astype(F32)
    pair_cot_b = by_core(both_kept[tok_share:], both_got[tok_share:], 0)
    pair_cot = pair_cot_b.astype(F32)
    gain = own_half(norm_gain, 0)[None, :]

    entering = combine_states(exchange_states(local_state), seq_place - 1 - peers)
    entering_b = entering.astype(BF16)
    scores = heads_dot("htd,hsd->hts", query_heads, key_heads) * decay_band
    scores_b = scores.astype(BF16)
    attended = heads_dot("hts,hse->hte", scores_b, value_heads)
    attended = attended + head_decay * heads_dot("htd,hde->hte", query_heads, entering_b)
    attended_b = from_heads(attended).astype(BF16)

    out_own, out_other = own_half(w_out, 1), other_half(w_out, 1)
    got = swap(mm(attended_b, out_other).astype(BF16))
    chip_mixed = (mm(attended_b, out_own) + got.astype(F32)).astype(BF16)
    quarters = pair_cot_b.reshape(pair_share, 2, half // 2).transpose(1, 0, 2)
    quarters = jnp.broadcast_to(quarters[None], (z_count // 2,) + quarters.shape)
    sent = jnp.concatenate(
        [
            chip_mixed.reshape(z_count, pair_share, half),
            quarters.reshape(z_count, pair_share, half // 2),
        ],
        axis=2,
    )
    arrived = lax.all_to_all(sent, "mp", 0, 0, axis_index_groups=z_groups, tiled=True)
    stream = pair_inputs + jnp.sum(arrived[:, :, :half].astype(F32), axis=0)
    block_cot = arrived[:, :, half:].reshape(length, half // 2)

    def over_features(x):
        total = jnp.sum(x, axis=1, keepdims=True)
        return lax.psum(total, "mp", axis_index_groups=core_groups) / width


    stream_b = stream.astype(BF16)
    weights_kept, weights_got, stream_b = lax.optimization_barrier(
        (weights_kept, weights_got, stream_b)
    )
    both_weights = jnp.concatenate(
        [weights_kept[: 2 * hidden_units], weights_got[: 2 * hidden_units]], axis=0
    )
    block_stream = spread_z(stream_b).astype(F32)
    block_inverse = lax.rsqrt(over_features(block_stream * block_stream) + EPSILON)
    group_in = (block_stream * block_inverse * gain).astype(BF16)
    inverse = lax.dynamic_slice_in_dim(
        block_inverse, lax.axis_index("mp") // 2 * pair_share, pair_share, 0
    )
    normed = stream * inverse
    outgoing = mm(placing, group_in).astype(BF16).reshape(seq_count, capacity, half)
    weighted = (slot_weight.reshape(-1, 1) * mm(placing, block_cot)).astype(BF16)
    cot_own = lax.all_to_all(
        weighted.reshape(seq_count, capacity, half // 2), "seq", 0, 0, tiled=True
    ).reshape(-1, half // 2)
    cot_own, outgoing = lax.optimization_barrier((cot_own, outgoing))
    cot_pair = across_z(cot_own, 1)
    rows = lax.all_to_all(outgoing, "seq", 0, 0, tiled=True).reshape(-1, half)

    def features_part(part):
        pre = mm_t(part[: 2 * hidden_units], rows)
        down = part[2 * hidden_units :]
        hidden = mm_t(own_quarter(down), cot_own) + mm_t(other_quarter(down), cot_pair)
        return jnp.concatenate([pre, hidden], axis=0)

    got = swap(features_part(weights_got))
    pre = features_part(weights_kept) + got
    gate_pre, up_pre = pre[:hidden_units], pre[hidden_units : 2 * hidden_units]
    hidden_grad = pre[2 * hidden_units :]
    sigma = jax.nn.sigmoid(gate_pre)
    gate_grad = (hidden_grad * up_pre * sigma * (1.0 + gate_pre * (1.0 - sigma))).astype(BF16)
    up_grad = (hidden_grad * gate_pre * sigma).astype(BF16)
    grads = jnp.concatenate([gate_grad, up_grad], axis=0)
    grads_got = swap(grads)

    slots = lax.dot_general(
        jnp.concatenate([grads, grads_got], axis=0),
        both_weights,
        (((0,), (0,)), ((), ())),
        preferred_element_type=F32,
    )
    slots = slots.astype(BF16).reshape(seq_count, capacity, half)

    returned = lax.all_to_all(slots, "seq", 0, 0, tiled=True).reshape(-1, half)
    token_part = lax.dot_general(
        placing, returned, (((0,), (0,)), ((), ())), preferred_element_type=F32
    )
    expert_grad = sum_z(token_part.astype(BF16))
    scaled = expert_grad * gain
    stream_grad = inverse * (scaled - normed * over_features(scaled * normed)) + pair_cot
    pair_grad = stream_grad.astype(BF16)

    block_own = spread_z(pair_grad)
    block_other = swap(block_own)
    attended_grad = mm_t(block_own, out_own) + mm_t(block_other, out_other)
    grad_heads = to_heads(attended_grad)
    grad_b = grad_heads.astype(BF16)
    local_adjoint = heads_dot(
        "htd,hte->hde",
        query_heads,
        (jnp.exp(-decay_rates[:, None] * (places + 1.0)[None, :])[:, :, None] * grad_heads).astype(BF16),
    ).astype(BF16)
    local_adjoint = local_adjoint.reshape(head_count * head_size, head_size)
    local_adjoint = jnp.broadcast_to(local_adjoint[None], (seq_count,) + local_adjoint.shape)
    adjoints = exchange_states(local_adjoint)
    grad_scores = (heads_dot("hte,hse->hts", grad_b, value_heads) * decay_band).astype(BF16)
    query_part = heads_dot("hts,hsd->htd", grad_scores, key_heads)
    query_part = query_part + head_decay * heads_dot("hte,hde->htd", grad_b, entering_b)
    key_part = heads_dot("hts,htd->hsd", grad_scores, query_heads)
    value_part = heads_dot("hts,hte->hse", scores_b, grad_b)
    query_grad = from_heads(query_part).astype(BF16)
    key_grad, value_grad = last_grads(
        decay_rates,
        seq_place,
        adjoints,
        key_rows,
        value_rows,
        from_heads(key_part),
        from_heads(value_part),
    )

    def own_tokens(x):
        return lax.dynamic_slice_in_dim(x, lax.axis_index("mp") * tok_share, tok_share, 0)

    input_grad = by_core(own_tokens(block_own), own_tokens(block_other), 1)
    return (query_grad, key_grad, value_grad, input_grad)


def solution(mesh):
    placed = (
        P("seq", "mp"),
        P("seq", "mp"),
        P("seq", "mp"),
        P("mp"),
        P("mp", None),
        P(("seq", "mp"), None),
        P(("seq", "mp"), None),
        P(),
        P("seq", None),
        P("seq", None),
        P("seq", None, "mp"),
        P("seq", None, "mp"),
        P("seq", "mp", None),
    )
    return jax.shard_map(
        body,
        mesh=mesh,
        in_specs=placed,
        out_specs=(P("seq", "mp"), P("seq", "mp"), P("seq", "mp"), P(("seq", "mp"), None)),
        check_vma=False,
    )
```

```python
import jax
import jax.numpy as jnp
from jax import lax
from jax.experimental import pallas as pl
from jax.experimental.pallas import tpu as pltpu
from jax.sharding import PartitionSpec as P

EPSILON = 1e-06
F32 = jnp.float32
BF16 = jnp.bfloat16


def mm(a, b):
    return jnp.dot(a, b, preferred_element_type=F32)


def mm_t(a, b):
    return lax.dot_general(a, b, (((1,), (1,)), ((), ())), preferred_element_type=F32)


def heads_dot(spec, a, b):
    return jnp.einsum(spec, a, b, preferred_element_type=F32)


LIMITS = pltpu.CompilerParams(vmem_limit_bytes=8 * 2**20)
VMEM = pl.BlockSpec(memory_space=pltpu.VMEM)
SMEM = pl.BlockSpec(memory_space=pltpu.SMEM)


def rows_of(length, lanes):
    return lax.broadcasted_iota(jnp.int32, (length, lanes), 0).astype(F32)


def state_kernel(head_size, first_power, step, rate_ref, left_ref, right_ref, out_ref):
    length = left_ref.shape[0]
    for head in range(rate_ref.shape[0]):
        columns = pl.ds(head * head_size, head_size)
        powers = first_power + step * rows_of(length, head_size)
        left = jnp.exp(-rate_ref[head] * powers) * left_ref[:, columns].astype(F32)
        state = lax.dot_general(
            left.astype(BF16),
            right_ref[:, columns].astype(BF16),
            (((0,), (0,)), ((), ())),
            preferred_element_type=F32,
        ).astype(BF16)
        for copy in range(out_ref.shape[0]):
            out_ref[copy, columns, :] = state


def state_copies(rates, left, right, copies, first_power, step):
    length, width = left.shape
    head_size = width // rates.shape[0]
    return pl.pallas_call(
        lambda *refs: state_kernel(head_size, first_power, step, *refs),
        out_shape=jax.ShapeDtypeStruct((copies, width, head_size), BF16),
        in_specs=[SMEM, VMEM, VMEM],
        out_specs=VMEM,
        cost_estimate=pl.CostEstimate(
            flops=2 * length * width * head_size,
            bytes_accessed=2 * (copies * width * head_size + 2 * length * width),
            transcendentals=length * width,
        ),
    )(rates, left, right)


def last_kernel(
    rate_ref, place_ref, states_ref, key_ref, value_ref, key_in_ref, value_in_ref, key_ref_out, value_ref_out
):
    length, width = key_ref.shape
    peers, _, head_size = states_ref.shape
    for head in range(rate_ref.shape[0]):
        rate = rate_ref[head]
        columns = pl.ds(head * head_size, head_size)
        leaving = jnp.zeros((head_size, head_size), F32)
        for peer in range(peers):
            ahead = peer - 1 - place_ref[0]
            power = jnp.full((1, head_size), rate * length * jnp.maximum(ahead, 0).astype(F32))
            share = jnp.where(ahead >= 0, jnp.exp(-power), 0.0)
            leaving = leaving + share * states_ref[peer, columns, :].astype(F32)
        leaving = leaving.astype(BF16)
        tail = jnp.exp(-rate * (length - 1.0 - rows_of(length, head_size)))
        key_part = key_in_ref[:, columns] + tail * mm_t(value_ref[:, columns], leaving)
        value_part = value_in_ref[:, columns] + tail * mm(key_ref[:, columns], leaving)
        key_ref_out[:, columns] = key_part.astype(BF16)
        value_ref_out[:, columns] = value_part.astype(BF16)


def last_grads(rates, place, states, key_rows, value_rows, key_inside, value_inside):
    length, width = key_rows.shape
    out = jax.ShapeDtypeStruct((length, width), BF16)
    return pl.pallas_call(
        last_kernel,
        out_shape=(out, out),
        in_specs=[SMEM, SMEM, VMEM, VMEM, VMEM, VMEM, VMEM],
        out_specs=(VMEM, VMEM),
        compiler_params=LIMITS,
        cost_estimate=pl.CostEstimate(
            flops=4 * length * width * states.shape[2],
            bytes_accessed=2 * states.size + 16 * length * width,
            transcendentals=length * width,
        ),
    )(rates, place.reshape(1), states, key_rows, value_rows, key_inside, value_inside)


def body(
    queries,
    key_rows,
    value_rows,
    decay_rates,
    w_out,
    inputs,
    cotangent,
    norm_gain,
    expert_ids,
    gate_weights,
    w_gate,
    w_up,
    w_down,
):
    length = queries.shape[0]
    head_count = decay_rates.shape[0]
    head_size = queries.shape[1] // head_count
    width = w_out.shape[1]
    half = width // 2
    tok_share = inputs.shape[0]
    pair_share = 2 * tok_share
    seq_count = lax.axis_size("seq")
    mp_count = lax.axis_size("mp")
    z_count = mp_count // 2
    seq_place = lax.axis_index("seq")
    core = lax.rem(lax.axis_index("mp"), 2)
    z_groups = [[2 * k + c for k in range(z_count)] for c in range(2)]
    core_groups = [[2 * k, 2 * k + 1] for k in range(z_count)]
    swap_pairs = [(i, i ^ 1) for i in range(mp_count)]

    def swap(x):
        return lax.ppermute(x, "mp", swap_pairs)

    def own_half(x, axis):
        return lax.dynamic_slice_in_dim(x, core * half, half, axis)

    def other_half(x, axis):
        return lax.dynamic_slice_in_dim(x, (1 - core) * half, half, axis)

    def by_core(mine, theirs, axis):
        return jnp.where(
            core == 0,
            jnp.concatenate([mine, theirs], axis=axis),
            jnp.concatenate([theirs, mine], axis=axis),
        )

    def spread_z(x):
        copies = jnp.broadcast_to(x[None], (z_count,) + x.shape)
        out = lax.all_to_all(copies, "mp", 0, 0, axis_index_groups=z_groups, tiled=True)
        return out.reshape((z_count * x.shape[0],) + x.shape[1:])

    z_odd = lax.rem(lax.axis_index("mp") // 2, 2)

    def own_quarter(x):
        return lax.dynamic_slice_in_dim(x, z_odd * (half // 2), half // 2, 1)

    def other_quarter(x):
        return lax.dynamic_slice_in_dim(x, (1 - z_odd) * (half // 2), half // 2, 1)

    def across_z(x, offset):
        return lax.ppermute(x, "mp", [(i, i ^ (2 * offset)) for i in range(mp_count)])

    def sum_z(x):
        parts = x.reshape(z_count, pair_share, half)
        out = lax.all_to_all(parts, "mp", 0, 0, axis_index_groups=z_groups, tiled=True)
        return jnp.sum(out.astype(F32), axis=0)

    def to_heads(matrix):
        return matrix.reshape(length, head_count, head_size).transpose(1, 0, 2)

    def from_heads(blocks):
        return blocks.transpose(1, 0, 2).reshape(length, head_count * head_size)

    capacity = 4 * length // seq_count
    labels = jnp.arange(seq_count, dtype=jnp.int32)
    first_pick = expert_ids[:, 0:1] == labels[None, :]
    second_pick = expert_ids[:, 1:2] == labels[None, :]
    chosen = (first_pick | second_pick).astype(jnp.int32)
    weight = jnp.where(first_pick, gate_weights[:, 0:1], 0.0) + jnp.where(
        second_pick, gate_weights[:, 1:2], 0.0
    )
    ranking = jnp.cumsum(chosen, axis=0) - 1
    slot_ids = jnp.arange(capacity, dtype=jnp.int32)
    placed = (chosen.T[:, None, :] == 1) & (ranking.T[:, None, :] == slot_ids[None, :, None])
    placing = placed.astype(BF16).reshape(seq_count * capacity, length)
    slot_weight = jnp.sum(jnp.where(placed, weight.T[:, None, :], 0.0), axis=2)

    query_heads, key_heads, value_heads = map(to_heads, (queries, key_rows, value_rows))
    places = jnp.arange(length).astype(F32)
    offset = places[:, None] - places[None, :]
    causal = offset >= 0
    clipped = jnp.where(causal, offset, 0.0)
    decay_band = jnp.where(causal[None], jnp.exp(-decay_rates[:, None, None] * clipped[None]), 0.0)
    head_decay = jnp.exp(-decay_rates[:, None] * places[None, :])[:, :, None]

    def exchange_states(sent):
        return lax.all_to_all(sent, "seq", 0, 0, tiled=True)

    def combine_states(states, ahead):
        rate = decay_rates[:, None] * length * jnp.maximum(ahead, 0).astype(F32)[None, :]
        share = jnp.where(ahead[None, :] >= 0, jnp.exp(-rate), 0.0)
        states = states.reshape(seq_count, head_count, head_size, head_size).astype(F32)
        return jnp.sum(share.T[:, :, None, None] * states, axis=0)

    peers = jnp.arange(seq_count, dtype=jnp.int32)
    local_state = state_copies(
        decay_rates, key_rows, value_rows, seq_count, float(length), -1.0
    )

    both = jnp.concatenate([inputs, cotangent], axis=0)
    hidden_units = w_down.shape[1]
    both, gate_in, up_in, down_in, local_state = lax.optimization_barrier(
        (both, w_gate[0], w_up[0], w_down[0], local_state)
    )
    weights = jnp.concatenate([gate_in.T, up_in.T, down_in], axis=0)
    both_kept, both_got = own_half(both, 1), swap(other_half(both, 1))
    weights_kept, weights_got = lax.optimization_barrier(
        (own_half(weights, 1), swap(other_half(weights, 1)))
    )
    pair_inputs = by_core(both_kept[:tok_share], both_got[:tok_share], 0).astype(F32)
    pair_cot_b = by_core(both_kept[tok_share:], both_got[tok_share:], 0)
    pair_cot = pair_cot_b.astype(F32)
    gain = own_half(norm_gain, 0)[None, :]

    entering = combine_states(exchange_states(local_state), seq_place - 1 - peers)
    entering_b = entering.astype(BF16)
    scores = heads_dot("htd,hsd->hts", query_heads, key_heads) * decay_band
    scores_b = scores.astype(BF16)
    attended = heads_dot("hts,hse->hte", scores_b, value_heads)
    attended = attended + head_decay * heads_dot("htd,hde->hte", query_heads, entering_b)
    attended_b = from_heads(attended).astype(BF16)

    out_own, out_other = own_half(w_out, 1), other_half(w_out, 1)
    got = swap(mm(attended_b, out_other).astype(BF16))
    chip_mixed = (mm(attended_b, out_own) + got.astype(F32)).astype(BF16)
    quarters = pair_cot_b.reshape(pair_share, 2, half // 2).transpose(1, 0, 2)
    quarters = jnp.broadcast_to(quarters[None], (z_count // 2,) + quarters.shape)
    sent = jnp.concatenate(
        [
            chip_mixed.reshape(z_count, pair_share, half),
            quarters.reshape(z_count, pair_share, half // 2),
        ],
        axis=2,
    )
    arrived = lax.all_to_all(sent, "mp", 0, 0, axis_index_groups=z_groups, tiled=True)
    stream = pair_inputs + jnp.sum(arrived[:, :, :half].astype(F32), axis=0)
    block_cot = arrived[:, :, half:].reshape(length, half // 2)

    def over_features(x):
        total = jnp.sum(x, axis=1, keepdims=True)
        return lax.psum(total, "mp", axis_index_groups=core_groups) / width


    stream_b = stream.astype(BF16)
    weights_kept, weights_got, stream_b = lax.optimization_barrier(
        (weights_kept, weights_got, stream_b)
    )
    both_weights = jnp.concatenate(
        [weights_kept[: 2 * hidden_units], weights_got[: 2 * hidden_units]], axis=0
    )
    block_stream = spread_z(stream_b).astype(F32)
    block_inverse = lax.rsqrt(over_features(block_stream * block_stream) + EPSILON)
    group_in = (block_stream * block_inverse * gain).astype(BF16)
    inverse = lax.dynamic_slice_in_dim(
        block_inverse, lax.axis_index("mp") // 2 * pair_share, pair_share, 0
    )
    normed = stream * inverse
    outgoing = mm(placing, group_in).astype(BF16).reshape(seq_count, capacity, half)
    adjoint_decay = jnp.exp(-decay_rates[:, None] * (places + 1.0)[None, :])[:, :, None]
    first_token = lax.axis_index("mp") * tok_share
    outgoing, inverse, normed, adjoint_decay, first_token = lax.optimization_barrier(
        (outgoing, inverse, normed, adjoint_decay, first_token)
    )
    weighted = (slot_weight.reshape(-1, 1) * mm(placing, block_cot)).astype(BF16)
    cot_own = lax.all_to_all(
        weighted.reshape(seq_count, capacity, half // 2), "seq", 0, 0, tiled=True
    ).reshape(-1, half // 2)
    cot_own, outgoing = lax.optimization_barrier((cot_own, outgoing))
    cot_pair = across_z(cot_own, 1)
    rows = lax.all_to_all(outgoing, "seq", 0, 0, tiled=True).reshape(-1, half)

    def features_part(part):
        pre = mm_t(part[: 2 * hidden_units], rows)
        down = part[2 * hidden_units :]
        hidden = mm_t(own_quarter(down), cot_own) + mm_t(other_quarter(down), cot_pair)
        return jnp.concatenate([pre, hidden], axis=0)

    got = swap(features_part(weights_got))
    pre = features_part(weights_kept) + got
    gate_pre, up_pre = pre[:hidden_units], pre[hidden_units : 2 * hidden_units]
    hidden_grad = pre[2 * hidden_units :]
    sigma = jax.nn.sigmoid(gate_pre)
    gate_grad = (hidden_grad * up_pre * sigma * (1.0 + gate_pre * (1.0 - sigma))).astype(BF16)
    up_grad = (hidden_grad * gate_pre * sigma).astype(BF16)
    grads = jnp.concatenate([gate_grad, up_grad], axis=0)
    grads_got = swap(grads)

    slots = lax.dot_general(
        jnp.concatenate([grads, grads_got], axis=0),
        both_weights,
        (((0,), (0,)), ((), ())),
        preferred_element_type=F32,
    )
    slots = slots.astype(BF16).reshape(seq_count, capacity, half)

    returned = lax.all_to_all(slots, "seq", 0, 0, tiled=True).reshape(-1, half)
    token_part = lax.dot_general(
        placing, returned, (((0,), (0,)), ((), ())), preferred_element_type=F32
    )
    expert_grad = sum_z(token_part.astype(BF16))
    scaled = expert_grad * gain
    stream_grad = inverse * (scaled - normed * over_features(scaled * normed)) + pair_cot
    pair_grad = stream_grad.astype(BF16)

    block_own = spread_z(pair_grad)
    block_other = swap(block_own)
    attended_grad = mm_t(block_own, out_own) + mm_t(block_other, out_other)
    grad_heads = to_heads(attended_grad)
    grad_b = grad_heads.astype(BF16)
    local_adjoint = heads_dot(
        "htd,hte->hde",
        query_heads,
        (adjoint_decay * grad_heads).astype(BF16),
    ).astype(BF16)
    local_adjoint = local_adjoint.reshape(head_count * head_size, head_size)
    local_adjoint = jnp.broadcast_to(local_adjoint[None], (seq_count,) + local_adjoint.shape)
    adjoints = exchange_states(local_adjoint)
    grad_scores = (heads_dot("hte,hse->hts", grad_b, value_heads) * decay_band).astype(BF16)
    query_part = heads_dot("hts,hsd->htd", grad_scores, key_heads)
    query_part = query_part + head_decay * heads_dot("hte,hde->htd", grad_b, entering_b)
    key_part = heads_dot("hts,htd->hsd", grad_scores, query_heads)
    value_part = heads_dot("hts,hte->hse", scores_b, grad_b)
    query_grad = from_heads(query_part).astype(BF16)
    key_grad, value_grad = last_grads(
        decay_rates,
        seq_place,
        adjoints,
        key_rows,
        value_rows,
        from_heads(key_part),
        from_heads(value_part),
    )

    def own_tokens(x):
        return lax.dynamic_slice(
            x, (first_token, 0), (tok_share, half), allow_negative_indices=False
        )

    input_grad = by_core(own_tokens(block_own), own_tokens(block_other), 1)
    return (query_grad, key_grad, value_grad, input_grad)


def solution(mesh):
    placed = (
        P("seq", "mp"),
        P("seq", "mp"),
        P("seq", "mp"),
        P("mp"),
        P("mp", None),
        P(("seq", "mp"), None),
        P(("seq", "mp"), None),
        P(),
        P("seq", None),
        P("seq", None),
        P("seq", None, "mp"),
        P("seq", None, "mp"),
        P("seq", "mp", None),
    )
    return jax.shard_map(
        body,
        mesh=mesh,
        in_specs=placed,
        out_specs=(P("seq", "mp"), P("seq", "mp"), P("seq", "mp"), P(("seq", "mp"), None)),
        check_vma=False,
    )
```

```python
import jax
import jax.numpy as jnp
from jax import lax
from jax.experimental import pallas as pl
from jax.experimental.pallas import tpu as pltpu
from jax.sharding import PartitionSpec as P

EPSILON = 1e-06
F32 = jnp.float32
BF16 = jnp.bfloat16


def mm(a, b):
    return jnp.dot(a, b, preferred_element_type=F32)


def mm_t(a, b):
    return lax.dot_general(a, b, (((1,), (1,)), ((), ())), preferred_element_type=F32)


def heads_dot(spec, a, b):
    return jnp.einsum(spec, a, b, preferred_element_type=F32)


LIMITS = pltpu.CompilerParams(vmem_limit_bytes=8 * 2**20)
VMEM = pl.BlockSpec(memory_space=pltpu.VMEM)
SMEM = pl.BlockSpec(memory_space=pltpu.SMEM)


def rows_of(length, lanes):
    return lax.broadcasted_iota(jnp.int32, (length, lanes), 0).astype(F32)


def state_kernel(head_size, first_power, step, rate_ref, left_ref, right_ref, out_ref):
    length = left_ref.shape[0]
    for head in range(rate_ref.shape[0]):
        columns = pl.ds(head * head_size, head_size)
        powers = first_power + step * rows_of(length, head_size)
        left = jnp.exp(-rate_ref[head] * powers) * left_ref[:, columns].astype(F32)
        state = lax.dot_general(
            left.astype(BF16),
            right_ref[:, columns].astype(BF16),
            (((0,), (0,)), ((), ())),
            preferred_element_type=F32,
        ).astype(BF16)
        for copy in range(out_ref.shape[0]):
            out_ref[copy, columns, :] = state


def state_copies(rates, left, right, copies, first_power, step):
    length, width = left.shape
    head_size = width // rates.shape[0]
    return pl.pallas_call(
        lambda *refs: state_kernel(head_size, first_power, step, *refs),
        out_shape=jax.ShapeDtypeStruct((copies, width, head_size), BF16),
        in_specs=[SMEM, VMEM, VMEM],
        out_specs=VMEM,
        cost_estimate=pl.CostEstimate(
            flops=2 * length * width * head_size,
            bytes_accessed=2 * (copies * width * head_size + 2 * length * width),
            transcendentals=length * width,
        ),
    )(rates, left, right)


def last_kernel(
    rate_ref, place_ref, states_ref, key_ref, value_ref, key_in_ref, value_in_ref, key_ref_out, value_ref_out
):
    length, width = key_ref.shape
    peers, _, head_size = states_ref.shape
    for head in range(rate_ref.shape[0]):
        rate = rate_ref[head]
        columns = pl.ds(head * head_size, head_size)
        leaving = jnp.zeros((head_size, head_size), F32)
        for peer in range(peers):
            ahead = peer - 1 - place_ref[0]
            power = jnp.full((1, head_size), rate * length * jnp.maximum(ahead, 0).astype(F32))
            share = jnp.where(ahead >= 0, jnp.exp(-power), 0.0)
            leaving = leaving + share * states_ref[peer, columns, :].astype(F32)
        leaving = leaving.astype(BF16)
        tail = jnp.exp(-rate * (length - 1.0 - rows_of(length, head_size)))
        key_part = key_in_ref[:, columns] + tail * mm_t(value_ref[:, columns], leaving)
        value_part = value_in_ref[:, columns] + tail * mm(key_ref[:, columns], leaving)
        key_ref_out[:, columns] = key_part.astype(BF16)
        value_ref_out[:, columns] = value_part.astype(BF16)


def last_grads(rates, place, states, key_rows, value_rows, key_inside, value_inside):
    length, width = key_rows.shape
    out = jax.ShapeDtypeStruct((length, width), BF16)
    return pl.pallas_call(
        last_kernel,
        out_shape=(out, out),
        in_specs=[SMEM, SMEM, VMEM, VMEM, VMEM, VMEM, VMEM],
        out_specs=(VMEM, VMEM),
        compiler_params=LIMITS,
        cost_estimate=pl.CostEstimate(
            flops=4 * length * width * states.shape[2],
            bytes_accessed=2 * states.size + 16 * length * width,
            transcendentals=length * width,
        ),
    )(rates, place.reshape(1), states, key_rows, value_rows, key_inside, value_inside)


def body(
    queries,
    key_rows,
    value_rows,
    decay_rates,
    w_out,
    inputs,
    cotangent,
    norm_gain,
    expert_ids,
    gate_weights,
    w_gate,
    w_up,
    w_down,
):
    length = queries.shape[0]
    head_count = decay_rates.shape[0]
    head_size = queries.shape[1] // head_count
    width = w_out.shape[1]
    half = width // 2
    tok_share = inputs.shape[0]
    pair_share = 2 * tok_share
    seq_count = lax.axis_size("seq")
    mp_count = lax.axis_size("mp")
    z_count = mp_count // 2
    seq_place = lax.axis_index("seq")
    core = lax.rem(lax.axis_index("mp"), 2)
    z_groups = [[2 * k + c for k in range(z_count)] for c in range(2)]
    core_groups = [[2 * k, 2 * k + 1] for k in range(z_count)]
    swap_pairs = [(i, i ^ 1) for i in range(mp_count)]

    def swap(x):
        return lax.ppermute(x, "mp", swap_pairs)

    def own_half(x, axis):
        return lax.dynamic_slice_in_dim(x, core * half, half, axis)

    def other_half(x, axis):
        return lax.dynamic_slice_in_dim(x, (1 - core) * half, half, axis)

    def by_core(mine, theirs, axis):
        return jnp.where(
            core == 0,
            jnp.concatenate([mine, theirs], axis=axis),
            jnp.concatenate([theirs, mine], axis=axis),
        )

    def spread_z(x):
        copies = jnp.broadcast_to(x[None], (z_count,) + x.shape)
        out = lax.all_to_all(copies, "mp", 0, 0, axis_index_groups=z_groups, tiled=True)
        return out.reshape((z_count * x.shape[0],) + x.shape[1:])

    z_odd = lax.rem(lax.axis_index("mp") // 2, 2)

    def own_quarter(x):
        return lax.dynamic_slice_in_dim(x, z_odd * (half // 2), half // 2, 1)

    def other_quarter(x):
        return lax.dynamic_slice_in_dim(x, (1 - z_odd) * (half // 2), half // 2, 1)

    def across_z(x, offset):
        return lax.ppermute(x, "mp", [(i, i ^ (2 * offset)) for i in range(mp_count)])

    def sum_z(x):
        parts = x.reshape(z_count, pair_share, half)
        out = lax.all_to_all(parts, "mp", 0, 0, axis_index_groups=z_groups, tiled=True)
        return jnp.sum(out.astype(F32), axis=0)

    def to_heads(matrix):
        return matrix.reshape(length, head_count, head_size).transpose(1, 0, 2)

    def from_heads(blocks):
        return blocks.transpose(1, 0, 2).reshape(length, head_count * head_size)

    capacity = 4 * length // seq_count
    labels = jnp.arange(seq_count, dtype=jnp.int32)
    first_pick = expert_ids[:, 0:1] == labels[None, :]
    second_pick = expert_ids[:, 1:2] == labels[None, :]
    chosen = (first_pick | second_pick).astype(jnp.int32)
    weight = jnp.where(first_pick, gate_weights[:, 0:1], 0.0) + jnp.where(
        second_pick, gate_weights[:, 1:2], 0.0
    )
    ranking = jnp.cumsum(chosen, axis=0) - 1
    slot_ids = jnp.arange(capacity, dtype=jnp.int32)
    placed = (chosen.T[:, None, :] == 1) & (ranking.T[:, None, :] == slot_ids[None, :, None])
    placing = placed.astype(BF16).reshape(seq_count * capacity, length)
    slot_weight = jnp.sum(jnp.where(placed, weight.T[:, None, :], 0.0), axis=2)

    query_heads, key_heads, value_heads = map(to_heads, (queries, key_rows, value_rows))
    places = jnp.arange(length).astype(F32)
    offset = places[:, None] - places[None, :]
    causal = offset >= 0
    clipped = jnp.where(causal, offset, 0.0)
    decay_band = jnp.where(causal[None], jnp.exp(-decay_rates[:, None, None] * clipped[None]), 0.0)
    head_decay = jnp.exp(-decay_rates[:, None] * places[None, :])[:, :, None]

    def exchange_states(sent):
        return lax.all_to_all(sent, "seq", 0, 0, tiled=True)

    def combine_states(states, ahead):
        rate = decay_rates[:, None] * length * jnp.maximum(ahead, 0).astype(F32)[None, :]
        share = jnp.where(ahead[None, :] >= 0, jnp.exp(-rate), 0.0)
        states = states.reshape(seq_count, head_count, head_size, head_size).astype(F32)
        return jnp.sum(share.T[:, :, None, None] * states, axis=0)

    peers = jnp.arange(seq_count, dtype=jnp.int32)
    local_state = state_copies(
        decay_rates, key_rows, value_rows, seq_count, float(length), -1.0
    )

    hidden_units = w_down.shape[1]
    inputs, cotangent, gate_in, up_in, down_in, local_state = lax.optimization_barrier(
        (inputs, cotangent, w_gate[0], w_up[0], w_down[0], local_state)
    )
    weights = jnp.concatenate([gate_in.T, up_in.T, down_in], axis=0)
    weights_kept, weights_got = lax.optimization_barrier(
        (own_half(weights, 1), swap(other_half(weights, 1)))
    )
    pair_inputs = by_core(own_half(inputs, 1), swap(other_half(inputs, 1)), 0).astype(F32)
    pair_cot_b = by_core(own_half(cotangent, 1), swap(other_half(cotangent, 1)), 0)
    gain = own_half(norm_gain, 0)[None, :]

    states, pair_inputs, pair_cot_b = lax.optimization_barrier(
        (exchange_states(local_state), pair_inputs, pair_cot_b)
    )
    pair_cot = pair_cot_b.astype(F32)
    entering = combine_states(states, seq_place - 1 - peers)
    entering_b = entering.astype(BF16)
    scores = heads_dot("htd,hsd->hts", query_heads, key_heads) * decay_band
    scores_b = scores.astype(BF16)
    attended = heads_dot("hts,hse->hte", scores_b, value_heads)
    attended = attended + head_decay * heads_dot("htd,hde->hte", query_heads, entering_b)
    attended_b = from_heads(attended).astype(BF16)

    out_own, out_other = own_half(w_out, 1), other_half(w_out, 1)
    got = swap(mm(attended_b, out_other).astype(BF16))
    chip_mixed = (mm(attended_b, out_own) + got.astype(F32)).astype(BF16)
    quarters = pair_cot_b.reshape(pair_share, 2, half // 2).transpose(1, 0, 2)
    quarters = jnp.broadcast_to(quarters[None], (z_count // 2,) + quarters.shape)
    sent = jnp.concatenate(
        [
            chip_mixed.reshape(z_count, pair_share, half),
            quarters.reshape(z_count, pair_share, half // 2),
        ],
        axis=2,
    )
    arrived = lax.all_to_all(sent, "mp", 0, 0, axis_index_groups=z_groups, tiled=True)
    stream = pair_inputs + jnp.sum(arrived[:, :, :half].astype(F32), axis=0)
    block_cot = arrived[:, :, half:].reshape(length, half // 2)

    def over_features(x):
        total = jnp.sum(x, axis=1, keepdims=True)
        return lax.psum(total, "mp", axis_index_groups=core_groups) / width


    stream_b = stream.astype(BF16)
    weights_kept, weights_got, stream_b = lax.optimization_barrier(
        (weights_kept, weights_got, stream_b)
    )
    both_weights = jnp.concatenate(
        [weights_kept[: 2 * hidden_units], weights_got[: 2 * hidden_units]], axis=0
    )
    block_stream = spread_z(stream_b).astype(F32)
    block_inverse = lax.rsqrt(over_features(block_stream * block_stream) + EPSILON)
    group_in = (block_stream * block_inverse * gain).astype(BF16)
    inverse = lax.dynamic_slice_in_dim(
        block_inverse, lax.axis_index("mp") // 2 * pair_share, pair_share, 0
    )
    normed = stream * inverse
    outgoing = mm(placing, group_in).astype(BF16).reshape(seq_count, capacity, half)
    adjoint_decay = jnp.exp(-decay_rates[:, None] * (places + 1.0)[None, :])[:, :, None]
    first_token = lax.axis_index("mp") * tok_share
    outgoing, inverse, normed, adjoint_decay, first_token = lax.optimization_barrier(
        (outgoing, inverse, normed, adjoint_decay, first_token)
    )
    weighted = (slot_weight.reshape(-1, 1) * mm(placing, block_cot)).astype(BF16)
    cot_own = lax.all_to_all(
        weighted.reshape(seq_count, capacity, half // 2), "seq", 0, 0, tiled=True
    ).reshape(-1, half // 2)
    cot_own, outgoing = lax.optimization_barrier((cot_own, outgoing))
    cot_pair = across_z(cot_own, 1)
    rows = lax.all_to_all(outgoing, "seq", 0, 0, tiled=True).reshape(-1, half)

    def features_part(part):
        pre = mm_t(part[: 2 * hidden_units], rows)
        down = part[2 * hidden_units :]
        hidden = mm_t(own_quarter(down), cot_own) + mm_t(other_quarter(down), cot_pair)
        return jnp.concatenate([pre, hidden], axis=0)

    got = swap(features_part(weights_got))
    pre = features_part(weights_kept) + got
    gate_pre, up_pre = pre[:hidden_units], pre[hidden_units : 2 * hidden_units]
    hidden_grad = pre[2 * hidden_units :]
    sigma = jax.nn.sigmoid(gate_pre)
    gate_grad = (hidden_grad * up_pre * sigma * (1.0 + gate_pre * (1.0 - sigma))).astype(BF16)
    up_grad = (hidden_grad * gate_pre * sigma).astype(BF16)
    grads = jnp.concatenate([gate_grad, up_grad], axis=0)
    grads_got = swap(grads)

    slots = lax.dot_general(
        jnp.concatenate([grads, grads_got], axis=0),
        both_weights,
        (((0,), (0,)), ((), ())),
        preferred_element_type=F32,
    )
    slots = slots.astype(BF16).reshape(seq_count, capacity, half)

    returned = lax.all_to_all(slots, "seq", 0, 0, tiled=True).reshape(-1, half)
    token_part = lax.dot_general(
        placing, returned, (((0,), (0,)), ((), ())), preferred_element_type=F32
    )
    expert_grad = sum_z(token_part.astype(BF16))
    scaled = expert_grad * gain
    stream_grad = inverse * (scaled - normed * over_features(scaled * normed)) + pair_cot
    pair_grad = stream_grad.astype(BF16)

    block_own = spread_z(pair_grad)
    block_other = swap(block_own)
    attended_grad = mm_t(block_own, out_own) + mm_t(block_other, out_other)
    grad_heads = to_heads(attended_grad)
    grad_b = grad_heads.astype(BF16)
    local_adjoint = heads_dot(
        "htd,hte->hde",
        query_heads,
        (adjoint_decay * grad_heads).astype(BF16),
    ).astype(BF16)
    local_adjoint = local_adjoint.reshape(head_count * head_size, head_size)
    local_adjoint = jnp.broadcast_to(local_adjoint[None], (seq_count,) + local_adjoint.shape)
    adjoints = exchange_states(local_adjoint)
    grad_scores = (heads_dot("hte,hse->hts", grad_b, value_heads) * decay_band).astype(BF16)
    query_part = heads_dot("hts,hsd->htd", grad_scores, key_heads)
    query_part = query_part + head_decay * heads_dot("hte,hde->htd", grad_b, entering_b)
    key_part = heads_dot("hts,htd->hsd", grad_scores, query_heads)
    value_part = heads_dot("hts,hte->hse", scores_b, grad_b)
    query_grad = from_heads(query_part).astype(BF16)
    key_grad, value_grad = last_grads(
        decay_rates,
        seq_place,
        adjoints,
        key_rows,
        value_rows,
        from_heads(key_part),
        from_heads(value_part),
    )

    def own_tokens(x):
        return lax.dynamic_slice(
            x, (first_token, 0), (tok_share, half), allow_negative_indices=False
        )

    input_grad = by_core(own_tokens(block_own), own_tokens(block_other), 1)
    return (query_grad, key_grad, value_grad, input_grad)


def solution(mesh):
    placed = (
        P("seq", "mp"),
        P("seq", "mp"),
        P("seq", "mp"),
        P("mp"),
        P("mp", None),
        P(("seq", "mp"), None),
        P(("seq", "mp"), None),
        P(),
        P("seq", None),
        P("seq", None),
        P("seq", None, "mp"),
        P("seq", None, "mp"),
        P("seq", "mp", None),
    )
    return jax.shard_map(
        body,
        mesh=mesh,
        in_specs=placed,
        out_specs=(P("seq", "mp"), P("seq", "mp"), P("seq", "mp"), P(("seq", "mp"), None)),
        check_vma=False,
    )
```
